128 devices in a mesh: lat: 16 (over x, y), lon: 8 (over z, core).
Axes of the slice: x: 4, y: 4, z: 4, core: 2. Of those that a mesh axis runs over, the one named last changes fastest.
Arguments:
- state: bfloat16 [2, 64, 512, 1024], P(None, None, 'lat', 'lon'), may hold values from 3 to 5
- land_mask: int32 [512, 1024], P('lat', 'lon'), may hold values from 0 to 1, as said below
- conv_weight: bfloat16 [3, 3, 64, 64], replicated, may hold values from -0.25 to 0.25
- norm_gain: float32 [64], replicated, may hold values from 0.5 to 1.5
- batchnorm_bias: float32 [64], replicated, may hold values from -0.5 to 0.5
- cotangent: bfloat16 [2, 64, 512, 1024], P(None, None, 'lat', 'lon'), may hold values from -6 to 6
Outputs:
- activated: bfloat16 [2, 64, 512, 1024], P(None, None, 'lat', 'lon')
- state_grad: bfloat16 [2, 64, 512, 1024], P(None, None, 'lat', 'lon')
- weight_grad: float32 [3, 3, 64, 64], replicated
- gain_gradient: float32 [64], replicated
- bias_grad: float32 [64], replicated
The draws below stay inside these ranges and needn't reach their ends.
Inputs may be any that keep to these rules, and one draw needn't show every extreme that they name: `land_mask`: ocean pixels lie in whole 32 x 32 ocean blocks, with some land pixels among them; land blocks are all 0. The first block of every region of 32 x 128 pixels is an ocean block.
All inputs are finite; a program needn't handle non-finite values.
Results may differ from the reference program's by a relative error of at most 0.00105.
The reference program's roundings to bfloat16 on the way count: a program that leaves them out, or rounds other values in their place, can miss the bound.
Values may be sent and summed in bfloat16 or wider, within the bound.
A program may use at most 128 MiB of HBM per device.

```python
import jax
import jax.numpy as jnp
from jax import lax

C = 64
B = 2
BLOCK = 32
ROWS_DEV = 32
COLS_DEV = 128
NLAT_PIX = 512
NLON_PIX = 1024


def draw_land_mask(key, part):
    base = jax.random.fold_in(key, 7)
    key_block, key_pixel = jax.random.split(base)
    blocks_lat = NLAT_PIX // BLOCK
    blocks_lon = NLON_PIX // BLOCK
    codes = jax.random.randint(key_block, (blocks_lat, blocks_lon), 0, 16)
    lat_index = jnp.arange(blocks_lat, dtype=jnp.int32)
    lon_index = jnp.arange(blocks_lon, dtype=jnp.int32)
    thresh = 2 + lat_index * 10 // max(blocks_lat - 1, 1)
    ocean_block = (codes >= thresh[:, None]).astype(jnp.int32)
    first_lat = lat_index % (ROWS_DEV // BLOCK) == 0
    first_lon = lon_index % (COLS_DEV // BLOCK) == 0
    forced = jnp.logical_and(first_lat[:, None], first_lon[None, :]).astype(jnp.int32)
    ocean_block = jnp.maximum(ocean_block, forced)
    ocean_block = jnp.repeat(jnp.repeat(ocean_block, BLOCK, axis=0), BLOCK, axis=1)
    pixels = (jax.random.randint(key_pixel, (NLAT_PIX, NLON_PIX), 0, 8) != 0).astype(jnp.int32)
    return ocean_block * pixels


def level_of(rng, dims, shards, least, high):
    factor_of = 1.0
    for axis_at, parts in shards:
        draws = jax.random.uniform(jax.random.fold_in(jax.random.fold_in(rng, 6), axis_at), (parts,), jnp.float32, least / len(shards), high / len(shards))
        factor_of = factor_of * jnp.repeat(jnp.exp(draws), dims[axis_at] // parts).reshape((-1,) + (1,) * (len(dims) - 1 - axis_at))
    return factor_of


def centred(key, shape, scale, most, pieces=(), kind=jnp.bfloat16):
    loudness = level_of(key, shape, pieces, -0.22, 0.18) if pieces else 1.0
    result = jax.random.normal(key, shape, jnp.float32) * scale * loudness
    return jnp.minimum(jnp.maximum(result, -most), most).astype(kind)


def setup_inputs(seed: int = 0) -> dict:
    seeds = jax.random.split(jax.random.key(seed), 7)
    return {
        "state": jnp.clip(3.0 + 2.0 * jax.random.uniform(seeds[0], (B, C, NLAT_PIX, NLON_PIX), jnp.float32) ** level_of(seeds[0], (B, C, NLAT_PIX, NLON_PIX), ((2, 16), (3, 8)), -0.2, 0.2), 3.0, 5.0).astype(jnp.bfloat16),
        "land_mask": draw_land_mask(jax.random.fold_in(seeds[6], 71), 0),
        "conv_weight": centred(seeds[2], (3, 3, C, C), (9 * C) ** -0.5, 0.25),
        "norm_gain": jnp.clip(1.0 + 0.1 * jax.random.normal(seeds[3], (C,), jnp.float32), 0.5, 1.5),
        "batchnorm_bias": jnp.clip(jax.random.uniform(seeds[4], (C,), jnp.float32, -0.5, 0.5), -0.5, 0.5),
        "cotangent": centred(seeds[5], (B, C, NLAT_PIX, NLON_PIX), 1.0, 6.0, ((2, 16), (3, 8))),
    }


def wrap_pad(field):
    wrapped = jnp.concatenate([field[..., -1:], field, field[..., :1]], axis=3)
    zeros = jnp.zeros(wrapped.shape[:2] + (1, wrapped.shape[3]), wrapped.dtype)
    return jnp.concatenate([zeros, wrapped, zeros], axis=2)

def valid_conv(padded, kernel):
    return lax.conv_general_dilated(padded, kernel, (1, 1), 'VALID', dimension_numbers=('NCHW', 'HWIO', 'NCHW'), preferred_element_type=jnp.float32)

def kernel_grad(padded, grad):
    raw = lax.conv_general_dilated(padded, grad, (1, 1), 'VALID', dimension_numbers=('CNHW', 'IOHW', 'NCHW'), preferred_element_type=jnp.float32)
    return jnp.transpose(raw, (2, 3, 0, 1))

def reference(state, land_mask, conv_weight, norm_gain, batchnorm_bias, cotangent):
    maskf = land_mask.astype(jnp.float32)
    full_ocean_mask = maskf[None, None]
    masked = state * land_mask.astype(jnp.bfloat16)[None, None]
    padded = wrap_pad(masked)
    conv = valid_conv(padded, conv_weight)
    count = jnp.maximum(state.shape[0] * jnp.sum(maskf), 1.0)
    mean = lax.optimization_barrier(jnp.sum(conv * full_ocean_mask, axis=(0, 2, 3))) / count
    centered_deviation = conv - mean[None, :, None, None]
    var = lax.optimization_barrier(jnp.sum(centered_deviation * centered_deviation * full_ocean_mask, axis=(0, 2, 3))) / count
    inverse_stddev = lax.rsqrt(var + 1e-05)
    normalized_state = centered_deviation * inverse_stddev[None, :, None, None]
    batchnorm_gain = norm_gain[None, :, None, None]
    preactivation = batchnorm_gain * normalized_state + batchnorm_bias[None, :, None, None]
    sigmoid_pre = jax.nn.sigmoid(preactivation)
    activated = (preactivation * sigmoid_pre * full_ocean_mask).astype(jnp.bfloat16)
    slope = sigmoid_pre * (1.0 + preactivation * (1.0 - sigmoid_pre))
    preactivation_gradient = cotangent.astype(jnp.float32) * full_ocean_mask * slope
    bias_grad = lax.optimization_barrier(jnp.sum(preactivation_gradient, axis=(0, 2, 3)))
    gain_gradient = lax.optimization_barrier(jnp.sum(preactivation_gradient * normalized_state, axis=(0, 2, 3)))
    shifted_first = (norm_gain * bias_grad / count)[None, :, None, None]
    shifted_second = (norm_gain * gain_gradient / count)[None, :, None, None]
    convolution_gradient_map = (full_ocean_mask * inverse_stddev[None, :, None, None] * (batchnorm_gain * preactivation_gradient - shifted_first - normalized_state * shifted_second)).astype(jnp.bfloat16)
    weight_grad = kernel_grad(padded, convolution_gradient_map)
    flipped = jnp.transpose(conv_weight[::-1, ::-1], (0, 1, 3, 2))
    back = valid_conv(wrap_pad(convolution_gradient_map), flipped)
    state_grad = (back * full_ocean_mask).astype(jnp.bfloat16)
    return (activated, state_grad, weight_grad, gain_gradient, bias_grad)
```

```python
import jax
import jax.numpy as jnp
from jax import lax
from jax.experimental import pallas as pl
from jax.experimental.pallas import tpu as pltpu
from jax.sharding import PartitionSpec as P

BF = jnp.bfloat16
F32 = jnp.float32
MESH = pl.DeviceIdType.MESH
NT = (((1,), (1,)), ((), ()))


def peer_offsets():
    found = []
    for dx in range(4):
        for dy in range(4):
            for dz in range(4):
                for dc in range(2):
                    if dx or dy or dz or dc:
                        hops = sum(min(a, 4 - a) for a in (dx, dy, dz))
                        found.append((-hops, dx, dy, dz, dc))
    found.sort()
    return [t[1:] for t in found]


OFFSETS = peer_offsets()


def peer(lat, lon, offset):
    dx, dy, dz, dc = offset
    plat = lax.rem(lax.div(lat, 4) + dx, 4) * 4 + lax.rem(lat + dy, 4)
    plon = lax.rem(lax.div(lon, 2) + dz, 4) * 2 + lax.rem(lon + dc, 2)
    return plat, plon


def kernel(
    state, mask, weight, gain, bias, cot,
    act_out, sgrad_out, wgrad_out, gain_out, bias_out,
    xin, cin, aout, sout, xs, ds, cv, dp, ctm, actt, wf, wb, epx, epd, erx, erd,
    stat_src, stat_buf, grad_src, grad_buf, wsrc, wbuf, acc, wgat, cols, mrow,
    dma, hsx, hrx, hsd, hrd, gss, grs,
):
    lat = lax.axis_index("lat")
    lon = lax.axis_index("lon")
    me = lat * 8 + lon
    north, south = lax.rem(lat + 15, 16), lax.rem(lat + 1, 16)
    west, east = lax.rem(lon + 7, 8), lax.rem(lon + 1, 8)

    load_x = pltpu.make_async_copy(state, xin, dma.at[0])
    load_x.start()
    load_c = pltpu.make_async_copy(cot, cin, dma.at[1])
    load_c.start()
    barrier = pltpu.get_barrier_semaphore()
    for f in OFFSETS:
        pl.semaphore_signal(barrier, 1, device_id=peer(lat, lon, f), device_id_type=MESH)

    maskf = mask[...].astype(F32)
    mrow[...] = maskf
    mask_bf = maskf.astype(BF)
    n_local = 2.0 * jnp.sum(jnp.sum(maskf, axis=0, keepdims=True), axis=1, keepdims=True)

    taps = weight[...].reshape(576, 64)
    wt = jnp.transpose(taps.astype(F32), (1, 0)).astype(BF)
    zero = jnp.zeros((64, 192), BF)
    wf[0:64, :] = jnp.concatenate([wt, zero], axis=1)
    wf[64:128, :] = jnp.concatenate([zero, wt], axis=1)
    back = jnp.concatenate([weight[2 - t // 3, 2 - t % 3] for t in range(9)], axis=1)
    wb[0:64, :] = jnp.concatenate([back, zero], axis=1)
    wb[64:128, :] = jnp.concatenate([zero, back], axis=1)
    gb = jnp.concatenate([gain[...].reshape(1, 64), bias[...].reshape(1, 64)], axis=1)
    gg = jnp.concatenate([gain[...].reshape(1, 64), gain[...].reshape(1, 64)], axis=1)

    def column(row):
        return jnp.transpose(jnp.broadcast_to(row, (128, 128)), (1, 0))

    gbc = column(gb)
    cols[0:128, :] = gbc

    lane = lax.broadcasted_iota(jnp.int32, (64, 128), 1)

    def shifts_and_pack(buf, epack):
        packed = jnp.zeros((64, 128), BF)
        for b in range(2):
            half = pl.ds(b * 128, 128)
            for i in range(32):
                q = b * 32 + i
                base = (i + 1) * 192
                v = buf[base + 64:base + 128, half]
                buf[base:base + 64, half] = pltpu.roll(v, 1, 1)
                buf[base + 128:base + 192, half] = pltpu.roll(v, 127, 1)
                turned = pltpu.roll(v, (2 * q + 1) % 128, 1)
                packed = jnp.where(lax.div(lane, 2) == q, turned, packed)
        epack[...] = packed

    def halo_copies(buf, epack, erecv, ss, rs):
        row = lambda p: buf.at[pl.ds((p * 3 + 1) * 64, 64)]
        plan = [
            (row(1), row(33), (north, lon)),
            (row(32), row(0), (south, lon)),
            (epack, erecv.at[0], (lat, east)),
            (epack, erecv.at[1], (lat, west)),
            (epack, erecv.at[2], (south, east)),
            (epack, erecv.at[3], (south, west)),
            (epack, erecv.at[4], (north, east)),
            (epack, erecv.at[5], (north, west)),
        ]
        return [
            pltpu.make_async_remote_copy(
                src_ref=s, dst_ref=d, send_sem=ss.at[k], recv_sem=rs.at[k], device_id=t, device_id_type=MESH
            )
            for k, (s, d, t) in enumerate(plan)
        ]

    def insert(buf, p, b, joined, q):
        half = pl.ds(b * 128, 128)
        base = p * 192
        r = pltpu.roll(joined, (127 - 2 * q) % 128, 1)
        buf[base:base + 64, half] = jnp.where(lane == 0, r, buf[base:base + 64, half])
        buf[base + 128:base + 192, half] = jnp.where(lane == 127, r, buf[base + 128:base + 192, half])

    def join(left, right):
        return jnp.where(lax.rem(lane, 2) == 0, pltpu.roll(right, 127, 1), pltpu.roll(left, 1, 1))

    def finish_halo(buf, erecv):
        for p, keep in ((0, lat > 0), (33, lat < 15)):
            base = p * 192
            scale = jnp.where(keep, 1.0, 0.0).astype(F32)
            v = (buf[base + 64:base + 128, :].astype(F32) * scale).astype(BF)
            buf[base + 64:base + 128, :] = v
            for b in range(2):
                half = pl.ds(b * 128, 128)
                vb = v[:, b * 128:(b + 1) * 128]
                buf[base:base + 64, half] = pltpu.roll(vb, 1, 1)
                buf[base + 128:base + 192, half] = pltpu.roll(vb, 127, 1)
            left, right, i = (erecv[2], erecv[3], 31) if p == 0 else (erecv[4], erecv[5], 0)
            corner = (join(left, right).astype(F32) * scale).astype(BF)
            for b in range(2):
                insert(buf, p, b, corner, b * 32 + i)
        joined = join(erecv[0], erecv[1])
        for b in range(2):
            for i in range(32):
                insert(buf, i + 1, b, joined, b * 32 + i)

    def exchange(src, buf, sem):
        for f in OFFSETS:
            pltpu.make_async_remote_copy(
                src_ref=src, dst_ref=buf.at[me], send_sem=gss.at[sem], recv_sem=grs.at[sem],
                device_id=peer(lat, lon, f), device_id_type=MESH,
            ).start()

    def exchange_wait(buf, sem):
        pltpu.make_async_copy(buf.at[pl.ds(0, 127)], buf.at[pl.ds(0, 127)], grs.at[sem]).wait()
        pltpu.make_async_copy(buf.at[pl.ds(0, 127)], buf.at[pl.ds(0, 127)], gss.at[sem]).wait()

    load_x.wait()
    for b in range(2):
        t = jnp.transpose(xin[b] * mask_bf[None], (1, 0, 2))
        for i in range(32):
            xs[(i + 1) * 192 + 64:(i + 1) * 192 + 128, b * 128:(b + 1) * 128] = t[i]
    shifts_and_pack(xs, epx)

    pl.semaphore_wait(barrier, 127)
    halo_x = halo_copies(xs, epx, erx, hsx, hrx)
    for c in halo_x:
        c.start()
    load_c.wait()
    for b in range(2):
        t = jnp.transpose(cin[b] * mask_bf[None], (1, 0, 2))
        for i in range(32):
            ctm[i * 64:(i + 1) * 64, b * 128:(b + 1) * 128] = t[i]
    for c in halo_x:
        c.wait()
    finish_halo(xs, erx)

    first = jnp.zeros((64, 128), F32)
    for p in range(16):
        r = jnp.dot(wf[...], xs[p * 384:p * 384 + 768, :], preferred_element_type=F32)
        cv[p * 128:(p + 1) * 128, :] = r
        for h in range(2):
            m = mrow[2 * p + h:2 * p + h + 1, :]
            first = first + (r[h * 64:(h + 1) * 64, :128] + r[h * 64:(h + 1) * 64, 128:]) * m
    mean_here = jnp.sum(first, axis=1, keepdims=True) / jnp.maximum(n_local, 1.0)
    mean_here = jnp.broadcast_to(mean_here, (64, 128))
    second = jnp.zeros((64, 128), F32)
    for i in range(32):
        m = mrow[i:i + 1, :]
        for b in range(2):
            d = cv[i * 64:(i + 1) * 64, b * 128:(b + 1) * 128] - mean_here
            second = second + d * d * m
    row = jnp.sum(jnp.transpose(jnp.concatenate([first, second], axis=0), (1, 0)), axis=0, keepdims=True)
    stat_src[...] = jnp.concatenate([row, jnp.broadcast_to(n_local, (1, 128))], axis=0)
    exchange(stat_src, stat_buf, 0)
    stat_buf[me] = stat_src[...]
    exchange_wait(stat_buf, 0)
    sums = stat_buf[:, 0, :]
    counts = stat_buf[:, 1, :]
    total = jnp.sum(sums, axis=0, keepdims=True)
    count = jnp.maximum(jnp.sum(counts, axis=0, keepdims=True), 1.0)
    mean = total / count
    apart = sums / jnp.maximum(counts, 1.0) - mean
    between = jnp.sum(apart * apart * counts, axis=0, keepdims=True)
    var = (total + pltpu.roll(between, 64, 1)) / count
    low = lax.broadcasted_iota(jnp.int32, (1, 128), 1) < 64
    mi = column(jnp.where(low, mean, lax.rsqrt(var + 1e-05)))
    cols[128:256, :] = mi

    mean_c, inv_c, gain_c, bias_c = cols[128:192, :], cols[192:256, :], cols[0:64, :], cols[64:128, :]
    gsum = jnp.zeros((64, 128), F32)
    bsum = jnp.zeros((64, 128), F32)
    for i in range(32):
        for b in range(2):
            at = (pl.ds(i * 64, 64), pl.ds(b * 128, 128))
            xhat = (cv[at] - mean_c) * inv_c
            pre = gain_c * xhat + bias_c
            s = 1.0 / (1.0 + jnp.exp(-pre))
            actt[at] = (pre * s).astype(BF)
            d = ctm[at].astype(F32) * (s * (1.0 + pre * (1.0 - s)))
            dp[at] = d
            bsum = bsum + d
            gsum = gsum + d * xhat
    grad_src[...] = jnp.sum(jnp.transpose(jnp.concatenate([bsum, gsum], axis=0), (1, 0)), axis=0, keepdims=True)
    exchange(grad_src, grad_buf, 1)
    grad_buf[me] = grad_src[...]

    def native(src, b):
        t = src[:, b * 128:(b + 1) * 128].reshape(32, 64, 128)
        return jnp.transpose(t, (1, 0, 2)) * mask_bf[None]

    for b in range(2):
        aout[b] = native(actt, b)
    save_a = pltpu.make_async_copy(aout, act_out, dma.at[0])
    save_a.start()

    exchange_wait(grad_buf, 1)
    gtot = jnp.sum(grad_buf[:, 0, :], axis=0, keepdims=True)
    bias_out[...] = gtot[0, :64]
    gain_out[...] = pltpu.roll(gtot, 64, 1)[0, :64]
    sc = column(gg * gtot / count)
    cols[256:384, :] = sc
    sf_c, sg_c = cols[256:320, :], cols[320:384, :]

    for i in range(32):
        m = mrow[i:i + 1, :]
        for b in range(2):
            at = (pl.ds(i * 64, 64), pl.ds(b * 128, 128))
            xhat = (cv[at] - mean_c) * inv_c
            d = m * inv_c * (gain_c * dp[at] - sf_c - xhat * sg_c)
            ds[(i + 1) * 192 + 64:(i + 1) * 192 + 128, b * 128:(b + 1) * 128] = d.astype(BF)
    shifts_and_pack(ds, epd)
    halo_d = halo_copies(ds, epd, erd, hsd, hrd)
    for c in halo_d:
        c.start()

    for p in range(8):
        right = jnp.concatenate(
            [ds[(4 * p + k + 1) * 192 + 64:(4 * p + k + 1) * 192 + 128, :] for k in range(4)], axis=0
        )
        part = lax.dot_general(xs[p * 768:p * 768 + 1152, :], right, NT, preferred_element_type=F32)
        if p == 0:
            acc[...] = part
        else:
            acc[...] += part
    here = []
    for ky in range(3):
        v = acc[ky * 192:(ky + 1) * 192, 0:64]
        for k in range(1, 4):
            v = v + acc[(ky + k) * 192:(ky + k + 1) * 192, k * 64:(k + 1) * 64]
        here.append(v)
    here = jnp.concatenate(here, axis=0)
    wsrc[...] = jnp.concatenate([here[:288], here[288:]], axis=1).reshape(72, 4, 128)

    def owner(la, lo):
        half = lax.rem(la, 2)
        return jnp.logical_or(half == 0, lo == 0), lax.div(la, 2) * 9 + half * 8 + lo

    own, mine = owner(lat, lon)
    for f in OFFSETS:
        la, lo = peer(lat, lon, f)
        owns, block = owner(la, lo)

        @pl.when(owns)
        def _():
            pltpu.make_async_remote_copy(
                src_ref=wsrc.at[block], dst_ref=wbuf.at[me], send_sem=gss.at[2], recv_sem=grs.at[2],
                device_id=(la, lo), device_id_type=MESH,
            ).start()

    @pl.when(own)
    def _():
        wbuf[me] = wsrc[mine]

    for c in halo_d:
        c.wait()
    finish_halo(ds, erd)
    for p in range(16):
        r = jnp.dot(wb[...], ds[p * 384:p * 384 + 768, :], preferred_element_type=F32)
        actt[p * 128:(p + 1) * 128, :] = r.astype(BF)
    for b in range(2):
        sout[b] = native(actt, b)
    save_s = pltpu.make_async_copy(sout, sgrad_out, dma.at[1])
    save_s.start()

    @pl.when(own)
    def _():
        pltpu.make_async_copy(wbuf.at[pl.ds(0, 127)], wbuf.at[pl.ds(0, 127)], grs.at[2]).wait()
        pltpu.make_async_copy(wsrc.at[pl.ds(0, 71)], wsrc.at[pl.ds(0, 71)], gss.at[2]).wait()
        wgat[mine] = jnp.sum(wbuf[...], axis=0)
        for f in OFFSETS:
            pltpu.make_async_remote_copy(
                src_ref=wgat.at[mine], dst_ref=wgat.at[mine], send_sem=gss.at[3], recv_sem=grs.at[3],
                device_id=peer(lat, lon, f), device_id_type=MESH,
            ).start()
        pltpu.make_async_copy(wgat.at[pl.ds(0, 71)], wgat.at[pl.ds(0, 71)], grs.at[3]).wait()
        pltpu.make_async_copy(wbuf.at[pl.ds(0, 127)], wbuf.at[pl.ds(0, 127)], gss.at[3]).wait()

    @pl.when(jnp.logical_not(own))
    def _():
        pltpu.make_async_copy(wsrc, wsrc, gss.at[2]).wait()
        pltpu.make_async_copy(wgat, wgat, grs.at[3]).wait()

    w = wgat[...].reshape(288, 128)
    wgrad_out[...] = jnp.concatenate([w[:, :64], w[:, 64:]], axis=0).reshape(3, 3, 64, 64)
    save_a.wait()
    save_s.wait()


def on_device(state, land_mask, conv_weight, norm_gain, batchnorm_bias, cotangent):
    vm = pl.BlockSpec(memory_space=pltpu.VMEM)
    anywhere = pl.BlockSpec(memory_space=pl.ANY)
    S = jax.ShapeDtypeStruct
    big = (2, 64, 32, 128)
    V = pltpu.VMEM
    return pl.pallas_call(
        kernel,
        out_shape=[S(big, BF), S(big, BF), S((3, 3, 64, 64), F32), S((64,), F32), S((64,), F32)],
        in_specs=[anywhere, vm, vm, vm, vm, anywhere],
        out_specs=[anywhere, anywhere, vm, vm, vm],
        scratch_shapes=[
            V(big, BF), V(big, BF), V(big, BF), V(big, BF),
            V((34 * 192, 256), BF), V((34 * 192, 256), BF),
            V((2048, 256), F32), V((2048, 256), F32), V((2048, 256), BF), V((2048, 256), BF),
            V((128, 768), BF), V((128, 768), BF),
            V((64, 128), BF), V((64, 128), BF), V((6, 64, 128), BF), V((6, 64, 128), BF),
            V((2, 128), F32), V((128, 2, 128), F32), V((1, 128), F32), V((128, 1, 128), F32),
            V((72, 4, 128), F32), V((128, 4, 128), F32), V((1152, 256), F32), V((72, 4, 128), F32),
            V((384, 128), F32), V((32, 128), F32),
            pltpu.SemaphoreType.DMA((2,)),
            pltpu.SemaphoreType.DMA((8,)), pltpu.SemaphoreType.DMA((8,)),
            pltpu.SemaphoreType.DMA((8,)), pltpu.SemaphoreType.DMA((8,)),
            pltpu.SemaphoreType.DMA((4,)), pltpu.SemaphoreType.DMA((4,)),
        ],
        compiler_params=pltpu.CompilerParams(
            collective_id=0, has_side_effects=True, vmem_limit_bytes=48 * 2**20
        ),
    )(state, land_mask, conv_weight, norm_gain, batchnorm_bias, cotangent)


def solution(mesh):
    return jax.shard_map(
        on_device,
        mesh=mesh,
        in_specs=(
            P(None, None, "lat", "lon"),
            P("lat", "lon"),
            P(),
            P(),
            P(),
            P(None, None, "lat", "lon"),
        ),
        out_specs=(P(None, None, "lat", "lon"), P(None, None, "lat", "lon"), P(), P(), P()),
        check_vma=False,
    )
```

```python
import jax
import jax.numpy as jnp
from jax import lax
from jax.experimental import pallas as pl
from jax.experimental.pallas import tpu as pltpu
from jax.sharding import PartitionSpec as P

BF = jnp.bfloat16
F32 = jnp.float32
MESH = pl.DeviceIdType.MESH
NT = (((1,), (1,)), ((), ()))


def peer_offsets():
    found = []
    for dx in range(4):
        for dy in range(4):
            for dz in range(4):
                for dc in range(2):
                    if dx or dy or dz or dc:
                        hops = sum(min(a, 4 - a) for a in (dx, dy, dz))
                        found.append((-hops, dx, dy, dz, dc))
    found.sort()
    return [t[1:] for t in found]


OFFSETS = peer_offsets()


def peer(lat, lon, offset):
    dx, dy, dz, dc = offset
    plat = lax.rem(lax.div(lat, 4) + dx, 4) * 4 + lax.rem(lat + dy, 4)
    plon = lax.rem(lax.div(lon, 2) + dz, 4) * 2 + lax.rem(lon + dc, 2)
    return plat, plon


def kernel(
    state, mask_hbm, weight_hbm, gain_hbm, bias_hbm, cot,
    aout, sout, wgrad_out, gain_out, bias_out,
    xin, cin, mask, weight, gain, bias, xs, ds, cv, dp, ctm, actt, wf, wb, epx, epd, erx, erd,
    stat_src, stat_buf, grad_src, grad_buf, wsrc, wbuf, acc, wgat, cols, mrow,
    dma, hsx, hrx, hsd, hrd, gss, grs,
):
    lat = lax.axis_index("lat")
    lon = lax.axis_index("lon")
    me = lat * 8 + lon
    north, south = lax.rem(lat + 15, 16), lax.rem(lat + 1, 16)
    west, east = lax.rem(lon + 7, 8), lax.rem(lon + 1, 8)

    loads = [
        pltpu.make_async_copy(s, d, dma.at[k])
        for k, (s, d) in enumerate(
            [(state, xin), (mask_hbm, mask), (weight_hbm, weight), (gain_hbm, gain), (bias_hbm, bias), (cot, cin)]
        )
    ]
    for c in loads:
        c.start()
    barrier = pltpu.get_barrier_semaphore()
    for f in OFFSETS:
        pl.semaphore_signal(barrier, 1, device_id=peer(lat, lon, f), device_id_type=MESH)

    for c in loads[1:5]:
        c.wait()
    maskf = mask[...].astype(F32)
    mrow[...] = maskf
    mask_bf = maskf.astype(BF)
    n_local = 2.0 * jnp.sum(jnp.sum(maskf, axis=0, keepdims=True), axis=1, keepdims=True)

    taps = weight[...].reshape(576, 64)
    wt = jnp.transpose(taps.astype(F32), (1, 0)).astype(BF)
    zero = jnp.zeros((64, 192), BF)
    wf[0:64, :] = jnp.concatenate([wt, zero], axis=1)
    wf[64:128, :] = jnp.concatenate([zero, wt], axis=1)
    back = jnp.concatenate([weight[2 - t // 3, 2 - t % 3] for t in range(9)], axis=1)
    wb[0:64, :] = jnp.concatenate([back, zero], axis=1)
    wb[64:128, :] = jnp.concatenate([zero, back], axis=1)
    gb = jnp.concatenate([gain[...].reshape(1, 64), bias[...].reshape(1, 64)], axis=1)
    gg = jnp.concatenate([gain[...].reshape(1, 64), gain[...].reshape(1, 64)], axis=1)

    def column(row):
        return jnp.transpose(jnp.broadcast_to(row, (128, 128)), (1, 0))

    gbc = column(gb)
    cols[0:128, :] = gbc

    lane = lax.broadcasted_iota(jnp.int32, (64, 128), 1)

    def shifts_and_pack(buf, epack):
        packed = jnp.zeros((64, 128), BF)
        for b in range(2):
            half = pl.ds(b * 128, 128)
            for i in range(32):
                q = b * 32 + i
                base = (i + 1) * 192
                v = buf[base + 64:base + 128, half]
                buf[base:base + 64, half] = pltpu.roll(v, 1, 1)
                buf[base + 128:base + 192, half] = pltpu.roll(v, 127, 1)
                turned = pltpu.roll(v, (2 * q + 1) % 128, 1)
                packed = jnp.where(lax.div(lane, 2) == q, turned, packed)
        epack[...] = packed

    def halo_copies(buf, epack, erecv, ss, rs):
        row = lambda p: buf.at[pl.ds((p * 3 + 1) * 64, 64)]
        plan = [
            (row(1), row(33), (north, lon)),
            (row(32), row(0), (south, lon)),
            (epack, erecv.at[0], (lat, east)),
            (epack, erecv.at[1], (lat, west)),
            (epack, erecv.at[2], (south, east)),
            (epack, erecv.at[3], (south, west)),
            (epack, erecv.at[4], (north, east)),
            (epack, erecv.at[5], (north, west)),
        ]
        return [
            pltpu.make_async_remote_copy(
                src_ref=s, dst_ref=d, send_sem=ss.at[k], recv_sem=rs.at[k], device_id=t, device_id_type=MESH
            )
            for k, (s, d, t) in enumerate(plan)
        ]

    def insert(buf, p, b, joined, q):
        half = pl.ds(b * 128, 128)
        base = p * 192
        r = pltpu.roll(joined, (127 - 2 * q) % 128, 1)
        buf[base:base + 64, half] = jnp.where(lane == 0, r, buf[base:base + 64, half])
        buf[base + 128:base + 192, half] = jnp.where(lane == 127, r, buf[base + 128:base + 192, half])

    def join(left, right):
        return jnp.where(lax.rem(lane, 2) == 0, pltpu.roll(right, 127, 1), pltpu.roll(left, 1, 1))

    def finish_halo(buf, erecv):
        for p, keep in ((0, lat > 0), (33, lat < 15)):
            base = p * 192
            scale = jnp.where(keep, 1.0, 0.0).astype(F32)
            v = (buf[base + 64:base + 128, :].astype(F32) * scale).astype(BF)
            buf[base + 64:base + 128, :] = v
            for b in range(2):
                half = pl.ds(b * 128, 128)
                vb = v[:, b * 128:(b + 1) * 128]
                buf[base:base + 64, half] = pltpu.roll(vb, 1, 1)
                buf[base + 128:base + 192, half] = pltpu.roll(vb, 127, 1)
            left, right, i = (erecv[2], erecv[3], 31) if p == 0 else (erecv[4], erecv[5], 0)
            corner = (join(left, right).astype(F32) * scale).astype(BF)
            for b in range(2):
                insert(buf, p, b, corner, b * 32 + i)
        joined = join(erecv[0], erecv[1])
        for b in range(2):
            for i in range(32):
                insert(buf, i + 1, b, joined, b * 32 + i)

    def exchange(src, buf, sem):
        for f in OFFSETS:
            pltpu.make_async_remote_copy(
                src_ref=src, dst_ref=buf.at[me], send_sem=gss.at[sem], recv_sem=grs.at[sem],
                device_id=peer(lat, lon, f), device_id_type=MESH,
            ).start()

    def exchange_wait(buf, sem):
        pltpu.make_async_copy(buf.at[pl.ds(0, 127)], buf.at[pl.ds(0, 127)], grs.at[sem]).wait()
        pltpu.make_async_copy(buf.at[pl.ds(0, 127)], buf.at[pl.ds(0, 127)], gss.at[sem]).wait()

    loads[0].wait()
    for b in range(2):
        t = jnp.transpose(xin[b] * mask_bf[None], (1, 0, 2))
        for i in range(32):
            xs[(i + 1) * 192 + 64:(i + 1) * 192 + 128, b * 128:(b + 1) * 128] = t[i]
    shifts_and_pack(xs, epx)

    pl.semaphore_wait(barrier, 127)
    halo_x = halo_copies(xs, epx, erx, hsx, hrx)
    for c in halo_x:
        c.start()
    loads[5].wait()
    for b in range(2):
        t = jnp.transpose(cin[b] * mask_bf[None], (1, 0, 2))
        for i in range(32):
            ctm[i * 64:(i + 1) * 64, b * 128:(b + 1) * 128] = t[i]
    for c in halo_x:
        c.wait()
    finish_halo(xs, erx)

    first = jnp.zeros((64, 128), F32)
    for p in range(16):
        r = jnp.dot(wf[...], xs[p * 384:p * 384 + 768, :], preferred_element_type=F32)
        cv[p * 128:(p + 1) * 128, :] = r
        for h in range(2):
            m = mrow[2 * p + h:2 * p + h + 1, :]
            first = first + (r[h * 64:(h + 1) * 64, :128] + r[h * 64:(h + 1) * 64, 128:]) * m
    mean_here = jnp.sum(first, axis=1, keepdims=True) / jnp.maximum(n_local, 1.0)
    mean_here = jnp.broadcast_to(mean_here, (64, 128))
    second = jnp.zeros((64, 128), F32)
    for i in range(32):
        m = mrow[i:i + 1, :]
        for b in range(2):
            d = cv[i * 64:(i + 1) * 64, b * 128:(b + 1) * 128] - mean_here
            second = second + d * d * m
    row = jnp.sum(jnp.transpose(jnp.concatenate([first, second], axis=0), (1, 0)), axis=0, keepdims=True)
    stat_src[...] = jnp.concatenate([row, jnp.broadcast_to(n_local, (1, 128))], axis=0)
    exchange(stat_src, stat_buf, 0)
    stat_buf[me] = stat_src[...]
    exchange_wait(stat_buf, 0)
    sums = stat_buf[:, 0, :]
    counts = stat_buf[:, 1, :]
    total = jnp.sum(sums, axis=0, keepdims=True)
    count = jnp.maximum(jnp.sum(counts, axis=0, keepdims=True), 1.0)
    mean = total / count
    apart = sums / jnp.maximum(counts, 1.0) - mean
    between = jnp.sum(apart * apart * counts, axis=0, keepdims=True)
    var = (total + pltpu.roll(between, 64, 1)) / count
    low = lax.broadcasted_iota(jnp.int32, (1, 128), 1) < 64
    mi = column(jnp.where(low, mean, lax.rsqrt(var + 1e-05)))
    cols[128:256, :] = mi

    mean_c, inv_c, gain_c, bias_c = cols[128:192, :], cols[192:256, :], cols[0:64, :], cols[64:128, :]
    gsum = jnp.zeros((64, 128), F32)
    bsum = jnp.zeros((64, 128), F32)
    for i in range(32):
        for b in range(2):
            at = (pl.ds(i * 64, 64), pl.ds(b * 128, 128))
            xhat = (cv[at] - mean_c) * inv_c
            pre = gain_c * xhat + bias_c
            s = 1.0 / (1.0 + jnp.exp(-pre))
            actt[at] = (pre * s).astype(BF)
            d = ctm[at].astype(F32) * (s * (1.0 + pre * (1.0 - s)))
            dp[at] = d
            bsum = bsum + d
            gsum = gsum + d * xhat
    grad_src[...] = jnp.sum(jnp.transpose(jnp.concatenate([bsum, gsum], axis=0), (1, 0)), axis=0, keepdims=True)
    exchange(grad_src, grad_buf, 1)
    grad_buf[me] = grad_src[...]

    def native(src, b):
        t = src[:, b * 128:(b + 1) * 128].reshape(32, 64, 128)
        return jnp.transpose(t, (1, 0, 2)) * mask_bf[None]

    for b in range(2):
        aout[b] = native(actt, b)

    exchange_wait(grad_buf, 1)
    gtot = jnp.sum(grad_buf[:, 0, :], axis=0, keepdims=True)
    bias_out[...] = gtot[0, :64]
    gain_out[...] = pltpu.roll(gtot, 64, 1)[0, :64]
    sc = column(gg * gtot / count)
    cols[256:384, :] = sc
    sf_c, sg_c = cols[256:320, :], cols[320:384, :]

    for i in range(32):
        m = mrow[i:i + 1, :]
        for b in range(2):
            at = (pl.ds(i * 64, 64), pl.ds(b * 128, 128))
            xhat = (cv[at] - mean_c) * inv_c
            d = m * inv_c * (gain_c * dp[at] - sf_c - xhat * sg_c)
            ds[(i + 1) * 192 + 64:(i + 1) * 192 + 128, b * 128:(b + 1) * 128] = d.astype(BF)
    for p in range(8):
        right = jnp.concatenate(
            [ds[(4 * p + k + 1) * 192 + 64:(4 * p + k + 1) * 192 + 128, :] for k in range(4)], axis=0
        )
        part = lax.dot_general(xs[p * 768:p * 768 + 1152, :], right, NT, preferred_element_type=F32)
        if p == 0:
            acc[...] = part
        else:
            acc[...] += part
    here = []
    for ky in range(3):
        v = acc[ky * 192:(ky + 1) * 192, 0:64]
        for k in range(1, 4):
            v = v + acc[(ky + k) * 192:(ky + k + 1) * 192, k * 64:(k + 1) * 64]
        here.append(v)
    here = jnp.concatenate(here, axis=0)
    wsrc[...] = jnp.concatenate([here[:288], here[288:]], axis=1).reshape(72, 4, 128)

    def owner(la, lo):
        half = lax.rem(la, 2)
        return jnp.logical_or(half == 0, lo == 0), lax.div(la, 2) * 9 + half * 8 + lo

    own, mine = owner(lat, lon)
    for f in OFFSETS:
        la, lo = peer(lat, lon, f)
        owns, block = owner(la, lo)

        @pl.when(owns)
        def _():
            pltpu.make_async_remote_copy(
                src_ref=wsrc.at[block], dst_ref=wbuf.at[me], send_sem=gss.at[2], recv_sem=grs.at[2],
                device_id=(la, lo), device_id_type=MESH,
            ).start()

    @pl.when(own)
    def _():
        wbuf[me] = wsrc[mine]

    shifts_and_pack(ds, epd)
    halo_d = halo_copies(ds, epd, erd, hsd, hrd)
    for c in halo_d:
        c.start()
    for c in halo_d:
        c.wait()
    finish_halo(ds, erd)
    for p in range(16):
        r = jnp.dot(wb[...], ds[p * 384:p * 384 + 768, :], preferred_element_type=F32)
        actt[p * 128:(p + 1) * 128, :] = r.astype(BF)
    @pl.when(own)
    def _():
        pltpu.make_async_copy(wbuf.at[pl.ds(0, 127)], wbuf.at[pl.ds(0, 127)], grs.at[2]).wait()
        wgat[mine] = jnp.sum(wbuf[...], axis=0)
        for f in OFFSETS:
            pltpu.make_async_remote_copy(
                src_ref=wgat.at[mine], dst_ref=wgat.at[mine], send_sem=gss.at[3], recv_sem=grs.at[3],
                device_id=peer(lat, lon, f), device_id_type=MESH,
            ).start()

    for b in range(2):
        sout[b] = native(actt, b)

    @pl.when(own)
    def _():
        pltpu.make_async_copy(wsrc.at[pl.ds(0, 71)], wsrc.at[pl.ds(0, 71)], gss.at[2]).wait()
        pltpu.make_async_copy(wgat.at[pl.ds(0, 71)], wgat.at[pl.ds(0, 71)], grs.at[3]).wait()
        pltpu.make_async_copy(wbuf.at[pl.ds(0, 127)], wbuf.at[pl.ds(0, 127)], gss.at[3]).wait()

    @pl.when(jnp.logical_not(own))
    def _():
        pltpu.make_async_copy(wsrc, wsrc, gss.at[2]).wait()
        pltpu.make_async_copy(wgat, wgat, grs.at[3]).wait()

    w = wgat[...].reshape(288, 128)
    wgrad_out[...] = jnp.concatenate([w[:, :64], w[:, 64:]], axis=0).reshape(3, 3, 64, 64)


def store(*refs):
    copies = [pltpu.make_async_copy(refs[k], refs[k + 5], refs[10].at[k]) for k in range(5)]
    for c in copies:
        c.start()
    for c in copies:
        c.wait()


def on_device(state, land_mask, conv_weight, norm_gain, batchnorm_bias, cotangent):
    vm = pl.BlockSpec(memory_space=pltpu.VMEM)
    hbm = pl.BlockSpec(memory_space=pltpu.HBM)
    anywhere = pl.BlockSpec(memory_space=pl.ANY)
    S = jax.ShapeDtypeStruct
    big = (2, 64, 32, 128)
    outs = [S(big, BF), S(big, BF), S((3, 3, 64, 64), F32), S((64,), F32), S((64,), F32)]
    V = pltpu.VMEM
    made = pl.pallas_call(
        kernel,
        out_shape=outs,
        in_specs=[hbm] * 6,
        out_specs=[vm] * 5,
        scratch_shapes=[
            V(big, BF), V(big, BF), V((32, 128), jnp.int32), V((3, 3, 64, 64), BF), V((64,), F32), V((64,), F32),
            V((34 * 192, 256), BF), V((34 * 192, 256), BF),
            V((2048, 256), F32), V((2048, 256), F32), V((2048, 256), BF), V((2048, 256), BF),
            V((128, 768), BF), V((128, 768), BF),
            V((64, 128), BF), V((64, 128), BF), V((6, 64, 128), BF), V((6, 64, 128), BF),
            V((2, 128), F32), V((128, 2, 128), F32), V((1, 128), F32), V((128, 1, 128), F32),
            V((72, 4, 128), F32), V((128, 4, 128), F32), V((1152, 256), F32), V((72, 4, 128), F32),
            V((384, 128), F32), V((32, 128), F32),
            pltpu.SemaphoreType.DMA((6,)),
            pltpu.SemaphoreType.DMA((8,)), pltpu.SemaphoreType.DMA((8,)),
            pltpu.SemaphoreType.DMA((8,)), pltpu.SemaphoreType.DMA((8,)),
            pltpu.SemaphoreType.DMA((4,)), pltpu.SemaphoreType.DMA((4,)),
        ],
        compiler_params=pltpu.CompilerParams(
            collective_id=0, has_side_effects=True, vmem_limit_bytes=40 * 2**20
        ),
    )(*[pltpu.with_memory_space_constraint(a, pltpu.HBM) for a in (state, land_mask, conv_weight, norm_gain, batchnorm_bias, cotangent)])
    return pl.pallas_call(
        store,
        out_shape=outs,
        in_specs=[vm] * 5,
        out_specs=[anywhere] * 5,
        scratch_shapes=[pltpu.SemaphoreType.DMA((5,))],
    )(*[pltpu.with_memory_space_constraint(a, pltpu.VMEM) for a in made])


def solution(mesh):
    return jax.shard_map(
        on_device,
        mesh=mesh,
        in_specs=(
            P(None, None, "lat", "lon"),
            P("lat", "lon"),
            P(),
            P(),
            P(),
            P(None, None, "lat", "lon"),
        ),
        out_specs=(P(None, None, "lat", "lon"), P(None, None, "lat", "lon"), P(), P(), P()),
        check_vma=False,
    )
```

```python
import jax
import jax.numpy as jnp
from jax import lax
from jax.experimental import pallas as pl
from jax.experimental.pallas import tpu as pltpu
from jax.sharding import PartitionSpec as P

BF = jnp.bfloat16
F32 = jnp.float32
MESH = pl.DeviceIdType.MESH
NT = (((1,), (1,)), ((), ()))


def peer_offsets():
    found = []
    for dx in range(4):
        for dy in range(4):
            for dz in range(4):
                for dc in range(2):
                    if dx or dy or dz or dc:
                        hops = sum(min(a, 4 - a) for a in (dx, dy, dz))
                        found.append((-hops, dx, dy, dz, dc))
    found.sort()
    return [t[1:] for t in found]


OFFSETS = peer_offsets()
FAR_XY = [(2, 2), (2, 1), (2, 3), (1, 2), (3, 2), (2, 0), (0, 2), (1, 1), (1, 3), (3, 1), (3, 3), (1, 0), (3, 0), (0, 1), (0, 3), (0, 0)]
GREETED = [(a, 0) for a in (10, 6, 2, 14, 9, 11, 5, 7, 8, 1, 3, 13, 15, 4, 12)]
GREETED = [(1, 1), (1, 7), (15, 1), (15, 7)] + GREETED + [(0, b) for b in (4, 5, 3, 2, 6, 1, 7)]


def kernel(
    state, mask_hbm, weight_hbm, gain_hbm, bias_hbm, cot,
    aout, sout, wgrad_out, gain_out, bias_out,
    xin, cin, mask, weight, gain, bias, xs, ds, cv, dp, ctm, actt, wf, wb, epx, epd, erx, erd,
    stat_src, stat_buf, grad_src, grad_buf, wsrc, wbuf, acc, wgat, cols, mrow,
    dma, hsx, hrx, hsd, hrd, gss, grs, all_here,
):
    lat = lax.axis_index("lat")
    lon = lax.axis_index("lon")
    me = lat * 8 + lon
    x, y, z, core = lax.div(lat, 4), lax.rem(lat, 4), lax.div(lon, 2), lax.rem(lon, 2)
    xs_at = [lax.rem(x + d, 4) for d in range(4)]
    ys_at = [lax.rem(y + d, 4) for d in range(4)]
    lats = [[xs_at[dx] * 4 + ys_at[dy] for dy in range(4)] for dx in range(4)]
    lons = [[lax.rem(z + d, 4) * 2 + lax.rem(core + c, 2) for c in range(2)] for d in range(4)]

    def peer(offset):
        dx, dy, dz, dc = offset
        return lats[dx][dy], lons[dz][dc]

    north, south = lax.rem(lat + 15, 16), lax.rem(lat + 1, 16)
    west, east = lax.rem(lon + 7, 8), lax.rem(lon + 1, 8)

    loads = [
        pltpu.make_async_copy(s, d, dma.at[k])
        for k, (s, d) in enumerate(
            [(state, xin), (mask_hbm, mask), (weight_hbm, weight), (gain_hbm, gain), (bias_hbm, bias), (cot, cin)]
        )
    ]
    for c in loads:
        c.start()
    barrier = pltpu.get_barrier_semaphore()
    for a, b in GREETED:
        there = (lax.rem(lat + a, 16), lax.rem(lon + b, 8))
        pl.semaphore_signal(barrier, 1, device_id=there, device_id_type=MESH)

    for c in loads[1:5]:
        c.wait()
    maskf = mask[...].astype(F32)
    mrow[...] = maskf
    mask_bf = maskf.astype(BF)
    n_local = 2.0 * jnp.sum(jnp.sum(maskf, axis=0, keepdims=True), axis=1, keepdims=True)

    taps = weight[...].reshape(576, 64)
    wt = jnp.transpose(taps.astype(F32), (1, 0)).astype(BF)
    zero = jnp.zeros((64, 192), BF)
    wf[0:64, :] = jnp.concatenate([wt, zero], axis=1)
    wf[64:128, :] = jnp.concatenate([zero, wt], axis=1)
    back = jnp.concatenate([weight[2 - t // 3, 2 - t % 3] for t in range(9)], axis=1)
    wb[0:64, :] = jnp.concatenate([back, zero], axis=1)
    wb[64:128, :] = jnp.concatenate([zero, back], axis=1)
    gb = jnp.concatenate([gain[...].reshape(1, 64), bias[...].reshape(1, 64)], axis=1)
    gg = jnp.concatenate([gain[...].reshape(1, 64), gain[...].reshape(1, 64)], axis=1)

    def column(row):
        return jnp.transpose(jnp.broadcast_to(row, (128, 128)), (1, 0))

    gbc = column(gb)
    cols[0:128, :] = gbc

    lane = lax.broadcasted_iota(jnp.int32, (64, 128), 1)

    def shifts_and_pack(buf, epack):
        packed = jnp.zeros((64, 128), BF)
        for b in range(2):
            half = pl.ds(b * 128, 128)
            for i in range(32):
                q = b * 32 + i
                base = (i + 1) * 192
                v = buf[base + 64:base + 128, half]
                buf[base:base + 64, half] = pltpu.roll(v, 1, 1)
                buf[base + 128:base + 192, half] = pltpu.roll(v, 127, 1)
                turned = pltpu.roll(v, (2 * q + 1) % 128, 1)
                packed = jnp.where(lax.div(lane, 2) == q, turned, packed)
        epack[...] = packed

    def halo_copies(buf, epack, erecv, ss, rs):
        row = lambda p: buf.at[pl.ds((p * 3 + 1) * 64, 64)]
        plan = [
            (row(1), row(33), (north, lon)),
            (row(32), row(0), (south, lon)),
            (epack, erecv.at[0], (lat, east)),
            (epack, erecv.at[1], (lat, west)),
            (epack, erecv.at[2], (south, east)),
            (epack, erecv.at[3], (south, west)),
            (epack, erecv.at[4], (north, east)),
            (epack, erecv.at[5], (north, west)),
        ]
        return [
            pltpu.make_async_remote_copy(
                src_ref=s, dst_ref=d, send_sem=ss.at[k], recv_sem=rs.at[k], device_id=t, device_id_type=MESH
            )
            for k, (s, d, t) in enumerate(plan)
        ]

    def insert(buf, p, b, joined, q):
        half = pl.ds(b * 128, 128)
        base = p * 192
        r = pltpu.roll(joined, (127 - 2 * q) % 128, 1)
        buf[base:base + 64, half] = jnp.where(lane == 0, r, buf[base:base + 64, half])
        buf[base + 128:base + 192, half] = jnp.where(lane == 127, r, buf[base + 128:base + 192, half])

    def join(left, right):
        return jnp.where(lax.rem(lane, 2) == 0, pltpu.roll(right, 127, 1), pltpu.roll(left, 1, 1))

    def finish_halo(buf, erecv):
        for p, keep in ((0, lat > 0), (33, lat < 15)):
            base = p * 192
            scale = jnp.where(keep, 1.0, 0.0).astype(F32)
            v = (buf[base + 64:base + 128, :].astype(F32) * scale).astype(BF)
            buf[base + 64:base + 128, :] = v
            for b in range(2):
                half = pl.ds(b * 128, 128)
                vb = v[:, b * 128:(b + 1) * 128]
                buf[base:base + 64, half] = pltpu.roll(vb, 1, 1)
                buf[base + 128:base + 192, half] = pltpu.roll(vb, 127, 1)
            left, right, i = (erecv[2], erecv[3], 31) if p == 0 else (erecv[4], erecv[5], 0)
            corner = (join(left, right).astype(F32) * scale).astype(BF)
            for b in range(2):
                insert(buf, p, b, corner, b * 32 + i)
        joined = join(erecv[0], erecv[1])
        for b in range(2):
            for i in range(32):
                insert(buf, i + 1, b, joined, b * 32 + i)

    def exchange(src, buf, sem):
        for f in OFFSETS:
            pltpu.make_async_remote_copy(
                src_ref=src, dst_ref=buf.at[me], send_sem=gss.at[sem], recv_sem=grs.at[sem],
                device_id=peer(f), device_id_type=MESH,
            ).start()

    def exchange_wait(buf, sem):
        pltpu.make_async_copy(buf.at[pl.ds(0, 127)], buf.at[pl.ds(0, 127)], grs.at[sem]).wait()
        pltpu.make_async_copy(buf.at[pl.ds(0, 127)], buf.at[pl.ds(0, 127)], gss.at[sem]).wait()

    loads[0].wait()
    for b in range(2):
        t = jnp.transpose(xin[b] * mask_bf[None], (1, 0, 2))
        for i in range(32):
            xs[(i + 1) * 192 + 64:(i + 1) * 192 + 128, b * 128:(b + 1) * 128] = t[i]
    shifts_and_pack(xs, epx)

    pl.semaphore_wait(barrier, len(GREETED))
    halo_x = halo_copies(xs, epx, erx, hsx, hrx)
    for c in halo_x:
        c.start()
    for a, b in GREETED:
        if a and not b:
            pl.semaphore_signal(all_here, 1, device_id=(lax.rem(lat + a, 16), lon), device_id_type=MESH)
    loads[5].wait()
    for b in range(2):
        t = jnp.transpose(cin[b] * mask_bf[None], (1, 0, 2))
        for i in range(32):
            ctm[i * 64:(i + 1) * 64, b * 128:(b + 1) * 128] = t[i]
    for c in halo_x:
        c.wait()
    finish_halo(xs, erx)

    first = jnp.zeros((64, 128), F32)
    for p in range(16):
        r = jnp.dot(wf[...], xs[p * 384:p * 384 + 768, :], preferred_element_type=F32)
        cv[p * 128:(p + 1) * 128, :] = r
        for h in range(2):
            m = mrow[2 * p + h:2 * p + h + 1, :]
            first = first + (r[h * 64:(h + 1) * 64, :128] + r[h * 64:(h + 1) * 64, 128:]) * m
    mean_here = jnp.sum(first, axis=1, keepdims=True) / jnp.maximum(n_local, 1.0)
    mean_here = jnp.broadcast_to(mean_here, (64, 128))
    second = jnp.zeros((64, 128), F32)
    for i in range(32):
        m = mrow[i:i + 1, :]
        for b in range(2):
            d = cv[i * 64:(i + 1) * 64, b * 128:(b + 1) * 128] - mean_here
            second = second + d * d * m
    row = jnp.sum(jnp.transpose(jnp.concatenate([first, second], axis=0), (1, 0)), axis=0, keepdims=True)
    stat_src[...] = jnp.concatenate([row, jnp.broadcast_to(n_local, (1, 128))], axis=0)
    pl.semaphore_wait(all_here, 15)
    exchange(stat_src, stat_buf, 0)
    stat_buf[me] = stat_src[...]
    exchange_wait(stat_buf, 0)
    sums = stat_buf[:, 0, :]
    counts = stat_buf[:, 1, :]
    total = jnp.sum(sums, axis=0, keepdims=True)
    count = jnp.maximum(jnp.sum(counts, axis=0, keepdims=True), 1.0)
    mean = total / count
    apart = sums / jnp.maximum(counts, 1.0) - mean
    between = jnp.sum(apart * apart * counts, axis=0, keepdims=True)
    var = (total + pltpu.roll(between, 64, 1)) / count
    low = lax.broadcasted_iota(jnp.int32, (1, 128), 1) < 64
    mi = column(jnp.where(low, mean, lax.rsqrt(var + 1e-05)))
    cols[128:256, :] = mi

    mean_c, inv_c, gain_c, bias_c = cols[128:192, :], cols[192:256, :], cols[0:64, :], cols[64:128, :]
    gsum = jnp.zeros((64, 128), F32)
    bsum = jnp.zeros((64, 128), F32)
    for i in range(32):
        for b in range(2):
            at = (pl.ds(i * 64, 64), pl.ds(b * 128, 128))
            xhat = (cv[at] - mean_c) * inv_c
            pre = gain_c * xhat + bias_c
            s = 1.0 / (1.0 + jnp.exp(-pre))
            actt[at] = (pre * s).astype(BF)
            d = ctm[at].astype(F32) * (s * (1.0 + pre * (1.0 - s)))
            dp[at] = d
            bsum = bsum + d
            gsum = gsum + d * xhat
    grad_src[...] = jnp.sum(jnp.transpose(jnp.concatenate([bsum, gsum], axis=0), (1, 0)), axis=0, keepdims=True)
    exchange(grad_src, grad_buf, 1)
    grad_buf[me] = grad_src[...]

    def native(src, b):
        t = src[:, b * 128:(b + 1) * 128].reshape(32, 64, 128)
        return jnp.transpose(t, (1, 0, 2)) * mask_bf[None]

    for b in range(2):
        aout[b] = native(actt, b)

    exchange_wait(grad_buf, 1)
    gtot = jnp.sum(grad_buf[:, 0, :], axis=0, keepdims=True)
    bias_out[...] = gtot[0, :64]
    gain_out[...] = pltpu.roll(gtot, 64, 1)[0, :64]
    sc = column(gg * gtot / count)
    cols[256:384, :] = sc
    sf_c, sg_c = cols[256:320, :], cols[320:384, :]

    for i in range(32):
        m = mrow[i:i + 1, :]
        for b in range(2):
            at = (pl.ds(i * 64, 64), pl.ds(b * 128, 128))
            xhat = (cv[at] - mean_c) * inv_c
            d = m * inv_c * (gain_c * dp[at] - sf_c - xhat * sg_c)
            ds[(i + 1) * 192 + 64:(i + 1) * 192 + 128, b * 128:(b + 1) * 128] = d.astype(BF)
    part_of = lax.rem(x + y + z, 4)
    own = part_of < 3
    mine = part_of * 32 + lat * 2 + core
    rows4 = [
        jnp.concatenate(
            [ds[(4 * p + k + 1) * 192 + 64:(4 * p + k + 1) * 192 + 128, :] for k in range(4)], axis=0
        )
        for p in range(8)
    ]
    for kx in range(3):
        for p in range(8):
            left = jnp.concatenate(
                [xs[(4 * p + k) * 192 + kx * 64:(4 * p + k) * 192 + kx * 64 + 64, :] for k in range(6)], axis=0
            )
            part = lax.dot_general(left, rows4[p], NT, preferred_element_type=F32)
            if p == 0:
                acc[...] = part
            else:
                acc[...] += part
        here = []
        for ky in range(3):
            v = acc[ky * 64:(ky + 1) * 64, 0:64]
            for k in range(1, 4):
                v = v + acc[(ky + k) * 64:(ky + k + 1) * 64, k * 64:(k + 1) * 64]
            here.append(v)
        here = jnp.concatenate(here, axis=0)
        wsrc[kx * 32:(kx + 1) * 32] = jnp.concatenate([here[:96], here[96:]], axis=1).reshape(32, 3, 128)
        for dx, dy in FAR_XY:
            for dc in (1, 0):
                la = lats[dx][dy]
                pc = lax.rem(core + dc, 2)
                lo = lax.rem(kx + 8 - xs_at[dx] - ys_at[dy], 4) * 2 + pc
                block = kx * 32 + la * 2 + pc
                send = pltpu.make_async_remote_copy(
                    src_ref=wsrc.at[block], dst_ref=wbuf.at[me], send_sem=gss.at[2], recv_sem=grs.at[2],
                    device_id=(la, lo), device_id_type=MESH,
                )
                if dx or dy or dc:
                    send.start()
                else:
                    pl.when(part_of != kx)(send.start)

    @pl.when(own)
    def _():
        wbuf[me] = wsrc[mine]

    shifts_and_pack(ds, epd)
    halo_d = halo_copies(ds, epd, erd, hsd, hrd)
    for c in halo_d:
        c.start()
    @pl.when(own)
    def _():
        pltpu.make_async_copy(wbuf.at[pl.ds(0, 127)], wbuf.at[pl.ds(0, 127)], grs.at[2]).wait()
        wgat[mine] = jnp.sum(wbuf[...], axis=0)
        for f in OFFSETS:
            pltpu.make_async_remote_copy(
                src_ref=wgat.at[mine], dst_ref=wgat.at[mine], send_sem=gss.at[3], recv_sem=grs.at[3],
                device_id=peer(f), device_id_type=MESH,
            ).start()

    for c in halo_d:
        c.wait()
    finish_halo(ds, erd)
    for p in range(16):
        r = jnp.dot(wb[...], ds[p * 384:p * 384 + 768, :], preferred_element_type=F32)
        actt[p * 128:(p + 1) * 128, :] = r.astype(BF)
    for b in range(2):
        sout[b] = native(actt, b)

    @pl.when(own)
    def _():
        pltpu.make_async_copy(wsrc.at[pl.ds(0, 95)], wsrc.at[pl.ds(0, 95)], gss.at[2]).wait()
        pltpu.make_async_copy(wgat.at[pl.ds(0, 95)], wgat.at[pl.ds(0, 95)], grs.at[3]).wait()
        pltpu.make_async_copy(wbuf.at[pl.ds(0, 127)], wbuf.at[pl.ds(0, 127)], gss.at[3]).wait()

    @pl.when(jnp.logical_not(own))
    def _():
        pltpu.make_async_copy(wsrc, wsrc, gss.at[2]).wait()
        pltpu.make_async_copy(wgat, wgat, grs.at[3]).wait()

    for kx in range(3):
        w = wgat[kx * 32:(kx + 1) * 32].reshape(96, 128)
        w = jnp.concatenate([w[:, :64], w[:, 64:]], axis=0)
        for ky in range(3):
            wgrad_out[ky, kx] = w[ky * 64:(ky + 1) * 64]


def store(*refs):
    copies = [pltpu.make_async_copy(refs[k], refs[k + 5], refs[10].at[k]) for k in range(5)]
    for c in copies:
        c.start()
    for c in copies:
        c.wait()


def on_device(state, land_mask, conv_weight, norm_gain, batchnorm_bias, cotangent):
    vm = pl.BlockSpec(memory_space=pltpu.VMEM)
    hbm = pl.BlockSpec(memory_space=pltpu.HBM)
    anywhere = pl.BlockSpec(memory_space=pl.ANY)
    S = jax.ShapeDtypeStruct
    big = (2, 64, 32, 128)
    outs = [S(big, BF), S(big, BF), S((3, 3, 64, 64), F32), S((64,), F32), S((64,), F32)]
    V = pltpu.VMEM
    made = pl.pallas_call(
        kernel,
        out_shape=outs,
        in_specs=[hbm] * 6,
        out_specs=[vm] * 5,
        scratch_shapes=[
            V(big, BF), V(big, BF), V((32, 128), jnp.int32), V((3, 3, 64, 64), BF), V((64,), F32), V((64,), F32),
            V((34 * 192, 256), BF), V((34 * 192, 256), BF),
            V((2048, 256), F32), V((2048, 256), F32), V((2048, 256), BF), V((2048, 256), BF),
            V((128, 768), BF), V((128, 768), BF),
            V((64, 128), BF), V((64, 128), BF), V((6, 64, 128), BF), V((6, 64, 128), BF),
            V((2, 128), F32), V((128, 2, 128), F32), V((1, 128), F32), V((128, 1, 128), F32),
            V((96, 3, 128), F32), V((128, 3, 128), F32), V((384, 256), F32), V((96, 3, 128), F32),
            V((384, 128), F32), V((32, 128), F32),
            pltpu.SemaphoreType.DMA((6,)),
            pltpu.SemaphoreType.DMA((8,)), pltpu.SemaphoreType.DMA((8,)),
            pltpu.SemaphoreType.DMA((8,)), pltpu.SemaphoreType.DMA((8,)),
            pltpu.SemaphoreType.DMA((4,)), pltpu.SemaphoreType.DMA((4,)),
            pltpu.SemaphoreType.REGULAR,
        ],
        compiler_params=pltpu.CompilerParams(
            collective_id=0, has_side_effects=True, vmem_limit_bytes=40 * 2**20
        ),
    )(*[pltpu.with_memory_space_constraint(a, pltpu.HBM) for a in (state, land_mask, conv_weight, norm_gain, batchnorm_bias, cotangent)])
    return pl.pallas_call(
        store,
        out_shape=outs,
        in_specs=[vm] * 5,
        out_specs=[anywhere] * 5,
        scratch_shapes=[pltpu.SemaphoreType.DMA((5,))],
    )(*[pltpu.with_memory_space_constraint(a, pltpu.VMEM) for a in made])


def solution(mesh):
    return jax.shard_map(
        on_device,
        mesh=mesh,
        in_specs=(
            P(None, None, "lat", "lon"),
            P("lat", "lon"),
            P(),
            P(),
            P(),
            P(None, None, "lat", "lon"),
        ),
        out_specs=(P(None, None, "lat", "lon"), P(None, None, "lat", "lon"), P(), P(), P()),
        check_vma=False,
    )
```

```python
import jax
import jax.numpy as jnp
from jax import lax
from jax.experimental import pallas as pl
from jax.experimental.pallas import tpu as pltpu
from jax.sharding import PartitionSpec as P

BF = jnp.bfloat16
F32 = jnp.float32
MESH = pl.DeviceIdType.MESH
NT = (((1,), (1,)), ((), ()))


def peer_offsets():
    found = []
    for dx in range(4):
        for dy in range(4):
            for dz in range(4):
                for dc in range(2):
                    if dx or dy or dz or dc:
                        hops = sum(min(a, 4 - a) for a in (dx, dy, dz))
                        found.append((-hops, dx, dy, dz, dc))
    found.sort()
    return [t[1:] for t in found]


OFFSETS = peer_offsets()
FAR_XY = [(2, 2), (2, 1), (2, 3), (1, 2), (3, 2), (2, 0), (0, 2), (1, 1), (1, 3), (3, 1), (3, 3), (1, 0), (3, 0), (0, 1), (0, 3), (0, 0)]
GREETED = [(a, 0) for a in (10, 6, 2, 14, 9, 11, 5, 7, 8, 1, 3, 13, 15, 4, 12)]
GREETED = [(1, 1), (1, 7), (15, 1), (15, 7)] + GREETED + [(0, b) for b in (4, 5, 3, 2, 6, 1, 7)]


def kernel(
    state, mask_hbm, weight_hbm, gain_hbm, bias_hbm, cot,
    aout, sout, wgrad_out, gain_out, bias_out,
    xin, cin, mask, weight, gain, bias, xs, ds, cv, dp, ctm, actt, wf, wb, wrow, wcol, rows4, epx, epd, erx, erd, cpx, cpd, crx, crd,
    stat_src, stat_buf, grad_src, grad_buf, wsrc, wbuf, acc, wgat, cols, mrow,
    dma, hsx, hrx, hsd, hrd, gss, grs, all_here,
):
    lat = lax.axis_index("lat")
    lon = lax.axis_index("lon")
    me = lat * 8 + lon
    x, y, z, core = lax.div(lat, 4), lax.rem(lat, 4), lax.div(lon, 2), lax.rem(lon, 2)
    xs_at = [lax.rem(x + d, 4) for d in range(4)]
    ys_at = [lax.rem(y + d, 4) for d in range(4)]
    lats = [[xs_at[dx] * 4 + ys_at[dy] for dy in range(4)] for dx in range(4)]
    lons = [[lax.rem(z + d, 4) * 2 + lax.rem(core + c, 2) for c in range(2)] for d in range(4)]

    def peer(offset):
        dx, dy, dz, dc = offset
        return lats[dx][dy], lons[dz][dc]

    north, south = lax.rem(lat + 15, 16), lax.rem(lat + 1, 16)
    west, east = lax.rem(lon + 7, 8), lax.rem(lon + 1, 8)

    loads = [
        pltpu.make_async_copy(s, d, dma.at[k])
        for k, (s, d) in enumerate(
            [(state, xin), (mask_hbm, mask), (weight_hbm, weight), (gain_hbm, gain), (bias_hbm, bias), (cot, cin)]
        )
    ]
    for c in loads:
        c.start()
    barrier = pltpu.get_barrier_semaphore()
    for a, b in GREETED:
        there = (lax.rem(lat + a, 16), lax.rem(lon + b, 8))
        pl.semaphore_signal(barrier, 1, device_id=there, device_id_type=MESH)

    for c in loads[1:5]:
        c.wait()
    maskf = mask[...].astype(F32)
    mrow[...] = maskf
    mask_bf = maskf.astype(BF)
    n_local = 2.0 * jnp.sum(jnp.sum(maskf, axis=0, keepdims=True), axis=1, keepdims=True)

    taps = weight[...].reshape(576, 64)
    wt = jnp.transpose(taps.astype(F32), (1, 0)).astype(BF)
    zero = jnp.zeros((64, 192), BF)
    wrow[0:64, :] = wt[:, 0:192]
    wrow[64:128, :] = wt[:, 384:576]
    wcol[0:64, :] = jnp.concatenate([wt[:, 192 * k + 128:192 * k + 192] for k in range(3)], axis=1)
    wcol[64:128, :] = jnp.concatenate([wt[:, 192 * k:192 * k + 64] for k in range(3)], axis=1)
    wf[0:64, :] = jnp.concatenate([wt, zero], axis=1)
    wf[64:128, :] = jnp.concatenate([zero, wt], axis=1)
    back = jnp.concatenate([weight[2 - t // 3, 2 - t % 3] for t in range(9)], axis=1)
    wb[0:64, :] = jnp.concatenate([back, zero], axis=1)
    wb[64:128, :] = jnp.concatenate([zero, back], axis=1)
    gb = jnp.concatenate([gain[...].reshape(1, 64), bias[...].reshape(1, 64)], axis=1)
    gg = jnp.concatenate([gain[...].reshape(1, 64), gain[...].reshape(1, 64)], axis=1)

    def column(row):
        return jnp.transpose(jnp.broadcast_to(row, (128, 128)), (1, 0))

    gbc = column(gb)
    cols[0:128, :] = gbc

    lane = lax.broadcasted_iota(jnp.int32, (64, 128), 1)

    def shifts_and_pack(buf, epack, cpack):
        packed = jnp.zeros((64, 128), BF)
        none = jnp.zeros((64, 128), BF)
        for b in range(2):
            half = pl.ds(b * 128, 128)
            for i in range(32):
                q = b * 32 + i
                base = (i + 1) * 192
                v = buf[base + 64:base + 128, half]
                buf[base:base + 64, half] = jnp.where(lane == 0, none, pltpu.roll(v, 1, 1))
                buf[base + 128:base + 192, half] = jnp.where(lane == 127, none, pltpu.roll(v, 127, 1))
                turned = pltpu.roll(v, (2 * q + 1) % 128, 1)
                packed = jnp.where(lax.div(lane, 2) == q, turned, packed)
        epack[...] = packed
        fold = jnp.zeros((16, 128), BF)
        for g in range(4):
            part = packed[16 * g:16 * g + 16]
            part = pltpu.roll(part, 4 * g, 1) if g else part
            pos = lax.rem(lane[0:16] + (128 - 4 * g), 128)
            corner = (pos < 2) | ((pos >= 62) & (pos < 66)) | (pos >= 126)
            fold = jnp.where(corner, part, fold)
        cpack[...] = fold

    def unfold(folded):
        return jnp.concatenate([folded] + [pltpu.roll(folded, 128 - 4 * g, 1) for g in range(1, 4)], axis=0)

    def halo_copies(buf, epack, cpack, erecv, crecv, ss, rs):
        row = lambda p: buf.at[pl.ds((p * 3 + 1) * 64, 64)]
        plan = [
            (cpack, crecv.at[0], (south, east)),
            (cpack, crecv.at[1], (south, west)),
            (cpack, crecv.at[2], (north, east)),
            (cpack, crecv.at[3], (north, west)),
            (row(1), row(33), (north, lon)),
            (row(32), row(0), (south, lon)),
            (epack, erecv.at[0], (lat, east)),
            (epack, erecv.at[1], (lat, west)),
        ]
        return [
            pltpu.make_async_remote_copy(
                src_ref=s, dst_ref=d, send_sem=ss.at[k], recv_sem=rs.at[k], device_id=t, device_id_type=MESH
            )
            for k, (s, d, t) in enumerate(plan)
        ]

    def insert(buf, p, b, joined, q):
        half = pl.ds(b * 128, 128)
        base = p * 192
        r = pltpu.roll(joined, (127 - 2 * q) % 128, 1)
        buf[base:base + 64, half] = jnp.where(lane == 0, r, buf[base:base + 64, half])
        buf[base + 128:base + 192, half] = jnp.where(lane == 127, r, buf[base + 128:base + 192, half])

    def join(left, right):
        return jnp.where(lax.rem(lane, 2) == 0, pltpu.roll(right, 127, 1), pltpu.roll(left, 1, 1))

    def finish_rows(buf, crecv):
        for p, keep in ((0, lat > 0), (33, lat < 15)):
            base = p * 192
            scale = jnp.where(keep, 1.0, 0.0).astype(F32)
            v = (buf[base + 64:base + 128, :].astype(F32) * scale).astype(BF)
            buf[base + 64:base + 128, :] = v
            for b in range(2):
                half = pl.ds(b * 128, 128)
                vb = v[:, b * 128:(b + 1) * 128]
                buf[base:base + 64, half] = pltpu.roll(vb, 1, 1)
                buf[base + 128:base + 192, half] = pltpu.roll(vb, 127, 1)
            left, right, i = (crecv[0], crecv[1], 31) if p == 0 else (crecv[2], crecv[3], 0)
            corner = (join(unfold(left), unfold(right)).astype(F32) * scale).astype(BF)
            for b in range(2):
                insert(buf, p, b, corner, b * 32 + i)

    def finish_columns(buf, erecv):
        joined = join(erecv[0], erecv[1])
        for b in range(2):
            for i in range(32):
                insert(buf, i + 1, b, joined, b * 32 + i)

    def exchange(src, buf, sem):
        for f in OFFSETS:
            pltpu.make_async_remote_copy(
                src_ref=src, dst_ref=buf.at[me], send_sem=gss.at[sem], recv_sem=grs.at[sem],
                device_id=peer(f), device_id_type=MESH,
            ).start()

    def exchange_wait(buf, sem):
        pltpu.make_async_copy(buf.at[pl.ds(0, 127)], buf.at[pl.ds(0, 127)], grs.at[sem]).wait()

    def exchange_sent(buf, sem):
        pltpu.make_async_copy(buf.at[pl.ds(0, 127)], buf.at[pl.ds(0, 127)], gss.at[sem]).wait()

    loads[0].wait()
    for b in range(2):
        t = jnp.transpose(xin[b] * mask_bf[None], (1, 0, 2))
        for i in range(32):
            xs[(i + 1) * 192 + 64:(i + 1) * 192 + 128, b * 128:(b + 1) * 128] = t[i]
    shifts_and_pack(xs, epx, cpx)

    pl.semaphore_wait(barrier, len(GREETED))
    halo_x = halo_copies(xs, epx, cpx, erx, crx, hsx, hrx)
    for c in halo_x:
        c.start()
    for a, b in GREETED:
        if a and not b:
            pl.semaphore_signal(all_here, 1, device_id=(lax.rem(lat + a, 16), lon), device_id_type=MESH)
    loads[5].wait()
    for b in range(2):
        t = jnp.transpose(cin[b] * mask_bf[None], (1, 0, 2))
        for i in range(32):
            ctm[i * 64:(i + 1) * 64, b * 128:(b + 1) * 128] = t[i]
    near = jnp.zeros((64, 128), F32)
    for p in range(16):
        if p == 0:
            r = jnp.dot(wf[:, 192:768], xs[192:768, :], preferred_element_type=F32)
        elif p == 15:
            r = jnp.dot(wf[:, 0:576], xs[30 * 192:33 * 192, :], preferred_element_type=F32)
        else:
            r = jnp.dot(wf[...], xs[p * 384:p * 384 + 768, :], preferred_element_type=F32)
        cv[p * 128:(p + 1) * 128, :] = r
        for h in range(2):
            m = mrow[2 * p + h:2 * p + h + 1, :]
            near = near + (r[h * 64:(h + 1) * 64, :128] + r[h * 64:(h + 1) * 64, 128:]) * m
    n_safe = jnp.maximum(n_local, 1.0)
    pivot = jnp.broadcast_to(jnp.sum(near, axis=1, keepdims=True) / n_safe, (64, 128))
    pivot_row = jnp.transpose(jnp.concatenate([pivot, jnp.zeros((64, 128), F32)], axis=0), (1, 0))[0:1]

    for c in halo_x:
        c.wait()
    finish_rows(xs, crx)
    top = jnp.dot(wrow[0:64, :], xs[0:192, :], preferred_element_type=F32)
    bottom = jnp.dot(wrow[64:128, :], xs[33 * 192:34 * 192, :], preferred_element_type=F32)
    joined = join(erx[0], erx[1])
    place = lax.rem(lax.div(lane, 2), 32)
    nothing = jnp.zeros((64, 128), BF)
    above = jnp.where(place == 0, nothing, pltpu.roll(joined, 2, 1))
    below = jnp.where(place == 31, nothing, pltpu.roll(joined, 126, 1))
    sides = jnp.dot(wcol[...], jnp.concatenate([above, joined, below], axis=0), preferred_element_type=F32)
    sides = jnp.where(lax.rem(lane, 2) == 0, sides[0:64], sides[64:128])
    edge = jnp.logical_or(lane == 0, lane == 127)
    first = jnp.zeros((64, 128), F32)
    second = jnp.zeros((64, 128), F32)
    for i in range(32):
        m = mrow[i:i + 1, :]
        for b in range(2):
            at = (pl.ds(i * 64, 64), pl.ds(b * 128, 128))
            side = pltpu.roll(sides, (127 - 2 * (b * 32 + i)) % 128, 1)
            v = cv[at] + jnp.where(edge, side, 0.0)
            if i == 0:
                v = v + top[:, b * 128:(b + 1) * 128]
            if i == 31:
                v = v + bottom[:, b * 128:(b + 1) * 128]
            cv[at] = v
            d = v - pivot
            md = d * m
            first = first + md
            second = second + d * md
    row = jnp.sum(jnp.transpose(jnp.concatenate([first, second], axis=0), (1, 0)), axis=0, keepdims=True)
    low = lax.broadcasted_iota(jnp.int32, (1, 128), 1) < 64
    sums_here = pltpu.roll(row, 64, 1)
    row = jnp.where(low, row + n_local * pivot_row, row - sums_here * sums_here / n_safe)
    stat_src[...] = jnp.concatenate([row, jnp.broadcast_to(n_local, (1, 128))], axis=0)
    pl.semaphore_wait(all_here, 15)
    exchange(stat_src, stat_buf, 0)
    stat_buf[me] = stat_src[...]
    finish_columns(xs, erx)
    exchange_wait(stat_buf, 0)
    sums = stat_buf[:, 0, :]
    counts = stat_buf[:, 1, :]
    total = jnp.sum(sums, axis=0, keepdims=True)
    count = jnp.maximum(jnp.sum(counts, axis=0, keepdims=True), 1.0)
    mean = total / count
    apart = sums / jnp.maximum(counts, 1.0) - mean
    between = jnp.sum(apart * apart * counts, axis=0, keepdims=True)
    var = (total + pltpu.roll(between, 64, 1)) / count
    mi = column(jnp.where(low, mean, lax.rsqrt(var + 1e-05)))
    cols[128:256, :] = mi

    mean_c, inv_c, gain_c, bias_c = cols[128:192, :], cols[192:256, :], cols[0:64, :], cols[64:128, :]
    gsum = jnp.zeros((64, 128), F32)
    bsum = jnp.zeros((64, 128), F32)
    for i in range(32):
        for b in range(2):
            at = (pl.ds(i * 64, 64), pl.ds(b * 128, 128))
            xhat = (cv[at] - mean_c) * inv_c
            pre = gain_c * xhat + bias_c
            s = 0.5 * jnp.tanh(0.5 * pre) + 0.5
            d = ctm[at].astype(F32) * (s * (1.0 + pre * (1.0 - s)))
            dp[at] = d
            bsum = bsum + d
            gsum = gsum + d * xhat
    grad_src[...] = jnp.sum(jnp.transpose(jnp.concatenate([bsum, gsum], axis=0), (1, 0)), axis=0, keepdims=True)
    exchange(grad_src, grad_buf, 1)
    grad_buf[me] = grad_src[...]

    def native(src, b):
        t = src[:, b * 128:(b + 1) * 128].reshape(32, 64, 128)
        return jnp.transpose(t, (1, 0, 2)) * mask_bf[None]

    for i in range(32):
        for b in range(2):
            at = (pl.ds(i * 64, 64), pl.ds(b * 128, 128))
            pre = gain_c * ((cv[at] - mean_c) * inv_c) + bias_c
            actt[at] = (pre * (0.5 * jnp.tanh(0.5 * pre) + 0.5)).astype(BF)
    for b in range(2):
        aout[b] = native(actt, b)

    exchange_wait(grad_buf, 1)
    gtot = jnp.sum(grad_buf[:, 0, :], axis=0, keepdims=True)
    bias_out[...] = gtot[0, :64]
    gain_out[...] = pltpu.roll(gtot, 64, 1)[0, :64]
    sc = column(gg * gtot / count)
    cols[256:384, :] = sc
    sf_c, sg_c = cols[256:320, :], cols[320:384, :]

    def left_rows(p, kx):
        return jnp.concatenate(
            [xs[(4 * p + k) * 192 + kx * 64:(4 * p + k) * 192 + kx * 64 + 64, :] for k in range(6)], axis=0
        )

    for i in range(32):
        m = mrow[i:i + 1, :]
        for b in range(2):
            at = (pl.ds(i * 64, 64), pl.ds(b * 128, 128))
            xhat = (cv[at] - mean_c) * inv_c
            d = m * inv_c * (gain_c * dp[at] - sf_c - xhat * sg_c)
            d = d.astype(BF)
            ds[(i + 1) * 192 + 64:(i + 1) * 192 + 128, b * 128:(b + 1) * 128] = d
            rows4[i * 64:(i + 1) * 64, b * 128:(b + 1) * 128] = d
        if i % 4 == 3:
            p = i // 4
            part = lax.dot_general(
                left_rows(p, 0), rows4[p * 256:(p + 1) * 256, :], NT, preferred_element_type=F32
            )
            if p == 0:
                acc[...] = part
            else:
                acc[...] += part
    part_of = lax.rem(x + y + z, 4)
    own = part_of < 3
    mine = part_of * 32 + lat * 2 + core
    for kx in range(3):
        for p in range(8 if kx else 0):
            part = lax.dot_general(
                left_rows(p, kx), rows4[p * 256:(p + 1) * 256, :], NT, preferred_element_type=F32
            )
            if p == 0:
                acc[...] = part
            else:
                acc[...] += part
        here = []
        for ky in range(3):
            v = acc[ky * 64:(ky + 1) * 64, 0:64]
            for k in range(1, 4):
                v = v + acc[(ky + k) * 64:(ky + k + 1) * 64, k * 64:(k + 1) * 64]
            here.append(v)
        here = jnp.concatenate(here, axis=0)
        here = jnp.concatenate([here[:96], here[96:]], axis=1)
        for k in range(3):
            wsrc[kx * 32:(kx + 1) * 32, k, :] = here[32 * k:32 * k + 32]
        for dx, dy in FAR_XY:
            for dc in (1, 0):
                la = lats[dx][dy]
                pc = lax.rem(core + dc, 2)
                lo = lax.rem(kx + 8 - xs_at[dx] - ys_at[dy], 4) * 2 + pc
                block = kx * 32 + la * 2 + pc
                send = pltpu.make_async_remote_copy(
                    src_ref=wsrc.at[block], dst_ref=wbuf.at[me], send_sem=gss.at[2], recv_sem=grs.at[2],
                    device_id=(la, lo), device_id_type=MESH,
                )
                if dx or dy or dc:
                    send.start()
                else:
                    pl.when(part_of != kx)(send.start)

    @pl.when(own)
    def _():
        wbuf[me] = wsrc[mine]

    shifts_and_pack(ds, epd, cpd)
    halo_d = halo_copies(ds, epd, cpd, erd, crd, hsd, hrd)
    for c in halo_d:
        c.start()
    @pl.when(own)
    def _():
        pltpu.make_async_copy(wbuf.at[pl.ds(0, 127)], wbuf.at[pl.ds(0, 127)], grs.at[2]).wait()
        quarters = [jnp.sum(wbuf[32 * k:32 * k + 32], axis=0) for k in range(4)]
        wgat[mine] = (quarters[0] + quarters[1]) + (quarters[2] + quarters[3])
        for f in OFFSETS:
            pltpu.make_async_remote_copy(
                src_ref=wgat.at[mine], dst_ref=wgat.at[mine], send_sem=gss.at[3], recv_sem=grs.at[3],
                device_id=peer(f), device_id_type=MESH,
            ).start()

    for c in halo_d:
        c.wait()
    finish_rows(ds, crd)
    finish_columns(ds, erd)
    for p in range(16):
        r = jnp.dot(wb[...], ds[p * 384:p * 384 + 768, :], preferred_element_type=F32)
        actt[p * 128:(p + 1) * 128, :] = r.astype(BF)
    for b in range(2):
        sout[b] = native(actt, b)

    @pl.when(own)
    def _():
        pltpu.make_async_copy(wsrc.at[pl.ds(0, 95)], wsrc.at[pl.ds(0, 95)], gss.at[2]).wait()
        pltpu.make_async_copy(wgat.at[pl.ds(0, 95)], wgat.at[pl.ds(0, 95)], grs.at[3]).wait()
        pltpu.make_async_copy(wbuf.at[pl.ds(0, 127)], wbuf.at[pl.ds(0, 127)], gss.at[3]).wait()

    @pl.when(jnp.logical_not(own))
    def _():
        pltpu.make_async_copy(wsrc, wsrc, gss.at[2]).wait()
        pltpu.make_async_copy(wgat, wgat, grs.at[3]).wait()

    exchange_sent(stat_buf, 0)
    exchange_sent(grad_buf, 1)
    for kx in range(3):
        w = jnp.concatenate([wgat[kx * 32:(kx + 1) * 32, k, :] for k in range(3)], axis=0)
        w = jnp.concatenate([w[:, :64], w[:, 64:]], axis=0)
        for ky in range(3):
            wgrad_out[ky, kx] = w[ky * 64:(ky + 1) * 64]


def store(*refs):
    copies = [pltpu.make_async_copy(refs[k], refs[k + 5], refs[10].at[k]) for k in range(5)]
    for c in copies:
        c.start()
    for c in copies:
        c.wait()


def on_device(state, land_mask, conv_weight, norm_gain, batchnorm_bias, cotangent):
    vm = pl.BlockSpec(memory_space=pltpu.VMEM)
    hbm = pl.BlockSpec(memory_space=pltpu.HBM)
    anywhere = pl.BlockSpec(memory_space=pl.ANY)
    S = jax.ShapeDtypeStruct
    big = (2, 64, 32, 128)
    outs = [S(big, BF), S(big, BF), S((3, 3, 64, 64), F32), S((64,), F32), S((64,), F32)]
    V = pltpu.VMEM
    made = pl.pallas_call(
        kernel,
        out_shape=outs,
        in_specs=[hbm] * 6,
        out_specs=[vm] * 5,
        scratch_shapes=[
            V(big, BF), V(big, BF), V((32, 128), jnp.int32), V((3, 3, 64, 64), BF), V((64,), F32), V((64,), F32),
            V((34 * 192, 256), BF), V((34 * 192, 256), BF),
            V((2048, 256), F32), V((2048, 256), F32), V((2048, 256), BF), V((2048, 256), BF),
            V((128, 768), BF), V((128, 768), BF), V((128, 192), BF), V((128, 192), BF), V((2048, 256), BF),
            V((64, 128), BF), V((64, 128), BF), V((2, 64, 128), BF), V((2, 64, 128), BF),
            V((16, 128), BF), V((16, 128), BF), V((4, 16, 128), BF), V((4, 16, 128), BF),
            V((2, 128), F32), V((128, 2, 128), F32), V((1, 128), F32), V((128, 1, 128), F32),
            V((96, 3, 128), F32), V((128, 3, 128), F32), V((384, 256), F32), V((96, 3, 128), F32),
            V((384, 128), F32), V((32, 128), F32),
            pltpu.SemaphoreType.DMA((6,)),
            pltpu.SemaphoreType.DMA((8,)), pltpu.SemaphoreType.DMA((8,)),
            pltpu.SemaphoreType.DMA((8,)), pltpu.SemaphoreType.DMA((8,)),
            pltpu.SemaphoreType.DMA((4,)), pltpu.SemaphoreType.DMA((4,)),
            pltpu.SemaphoreType.REGULAR,
        ],
        compiler_params=pltpu.CompilerParams(
            collective_id=0, has_side_effects=True, vmem_limit_bytes=40 * 2**20
        ),
    )(*[pltpu.with_memory_space_constraint(a, pltpu.HBM) for a in (state, land_mask, conv_weight, norm_gain, batchnorm_bias, cotangent)])
    return pl.pallas_call(
        store,
        out_shape=outs,
        in_specs=[vm] * 5,
        out_specs=[anywhere] * 5,
        scratch_shapes=[pltpu.SemaphoreType.DMA((5,))],
    )(*[pltpu.with_memory_space_constraint(a, pltpu.VMEM) for a in made])


def solution(mesh):
    return jax.shard_map(
        on_device,
        mesh=mesh,
        in_specs=(
            P(None, None, "lat", "lon"),
            P("lat", "lon"),
            P(),
            P(),
            P(),
            P(None, None, "lat", "lon"),
        ),
        out_specs=(P(None, None, "lat", "lon"), P(None, None, "lat", "lon"), P(), P(), P()),
        check_vma=False,
    )
```

```python
import jax
import jax.numpy as jnp
from jax import lax
from jax.experimental import pallas as pl
from jax.experimental.pallas import tpu as pltpu
from jax.sharding import PartitionSpec as P

BF = jnp.bfloat16
F32 = jnp.float32
MESH = pl.DeviceIdType.MESH
NT = (((1,), (1,)), ((), ()))


def peer_offsets():
    found = []
    for dx in range(4):
        for dy in range(4):
            for dz in range(4):
                for dc in range(2):
                    if dx or dy or dz or dc:
                        hops = sum(min(a, 4 - a) for a in (dx, dy, dz))
                        found.append((-hops, dx, dy, dz, dc))
    found.sort()
    return [t[1:] for t in found]


OFFSETS = peer_offsets()
FAR_XY = [(2, 2), (2, 1), (2, 3), (1, 2), (3, 2), (2, 0), (0, 2), (1, 1), (1, 3), (3, 1), (3, 3), (1, 0), (3, 0), (0, 1), (0, 3), (0, 0)]
GREETED = [(a, 0) for a in (10, 6, 2, 14, 9, 11, 5, 7, 8, 1, 3, 13, 15, 4, 12)]
GREETED = [(1, 1), (1, 7), (15, 1), (15, 7)] + GREETED + [(0, b) for b in (4, 5, 3, 2, 6, 1, 7)]


def kernel(
    state, mask_hbm, weight_hbm, gain_hbm, bias_hbm, cot,
    aout, sout, wgrad_out, gain_out, bias_out,
    xin, cin, mask, weight, gain, bias, xs, ds, cv, dp, ctm, actt, wf, wb, wrow, wcol, rows4, epx, epd, erx, erd, cpx, cpd, crx, crd,
    stat_src, stat_buf, grad_src, grad_buf, wsrc, wbuf, acc, wgat, cols, mrow,
    count_src, count_row, count_lon, count_lat,
    dma, hsx, hrx, hsd, hrd, gss, grs, cns, cnr, all_here,
):
    lat = lax.axis_index("lat")
    lon = lax.axis_index("lon")
    me = lat * 8 + lon
    x, y, z, core = lax.div(lat, 4), lax.rem(lat, 4), lax.div(lon, 2), lax.rem(lon, 2)
    xs_at = [lax.rem(x + d, 4) for d in range(4)]
    ys_at = [lax.rem(y + d, 4) for d in range(4)]
    lats = [[xs_at[dx] * 4 + ys_at[dy] for dy in range(4)] for dx in range(4)]
    lons = [[lax.rem(z + d, 4) * 2 + lax.rem(core + c, 2) for c in range(2)] for d in range(4)]

    def peer(offset):
        dx, dy, dz, dc = offset
        return lats[dx][dy], lons[dz][dc]

    north, south = lax.rem(lat + 15, 16), lax.rem(lat + 1, 16)
    west, east = lax.rem(lon + 7, 8), lax.rem(lon + 1, 8)

    loads = [
        pltpu.make_async_copy(s, d, dma.at[k])
        for k, (s, d) in enumerate(
            [(state, xin), (mask_hbm, mask), (weight_hbm, weight), (gain_hbm, gain), (bias_hbm, bias), (cot, cin)]
        )
    ]
    for c in loads:
        c.start()
    barrier = pltpu.get_barrier_semaphore()
    for a, b in GREETED:
        there = (lax.rem(lat + a, 16), lax.rem(lon + b, 8))
        pl.semaphore_signal(barrier, 1, device_id=there, device_id_type=MESH)

    for c in loads[1:5]:
        c.wait()
    maskf = mask[...].astype(F32)
    mrow[...] = maskf
    mask_bf = maskf.astype(BF)
    n_local = 2.0 * jnp.sum(jnp.sum(maskf, axis=0, keepdims=True), axis=1, keepdims=True)

    taps = weight[...].reshape(576, 64)
    wt = jnp.transpose(taps.astype(F32), (1, 0)).astype(BF)
    zero = jnp.zeros((64, 192), BF)
    wrow[0:64, :] = wt[:, 0:192]
    wrow[64:128, :] = wt[:, 384:576]
    wcol[0:64, :] = jnp.concatenate([wt[:, 192 * k + 128:192 * k + 192] for k in range(3)], axis=1)
    wcol[64:128, :] = jnp.concatenate([wt[:, 192 * k:192 * k + 64] for k in range(3)], axis=1)
    wf[0:64, :] = jnp.concatenate([wt, zero], axis=1)
    wf[64:128, :] = jnp.concatenate([zero, wt], axis=1)
    back = jnp.concatenate([weight[2 - t // 3, 2 - t % 3] for t in range(9)], axis=1)
    wb[0:64, :] = jnp.concatenate([back, zero], axis=1)
    wb[64:128, :] = jnp.concatenate([zero, back], axis=1)
    gb = jnp.concatenate([gain[...].reshape(1, 64), bias[...].reshape(1, 64)], axis=1)
    gg = jnp.concatenate([gain[...].reshape(1, 64), gain[...].reshape(1, 64)], axis=1)

    def column(row):
        return jnp.transpose(jnp.broadcast_to(row, (128, 128)), (1, 0))

    gbc = column(gb)
    cols[0:128, :] = gbc

    lane = lax.broadcasted_iota(jnp.int32, (64, 128), 1)

    def shifts_and_pack(buf, epack, cpack):
        packed = jnp.zeros((64, 128), BF)
        none = jnp.zeros((64, 128), BF)
        for b in range(2):
            half = pl.ds(b * 128, 128)
            for i in range(32):
                q = b * 32 + i
                base = (i + 1) * 192
                v = buf[base + 64:base + 128, half]
                buf[base:base + 64, half] = jnp.where(lane == 0, none, pltpu.roll(v, 1, 1))
                buf[base + 128:base + 192, half] = jnp.where(lane == 127, none, pltpu.roll(v, 127, 1))
                turned = pltpu.roll(v, (2 * q + 1) % 128, 1)
                packed = jnp.where(lax.div(lane, 2) == q, turned, packed)
        epack[...] = packed
        fold = jnp.zeros((16, 128), BF)
        for g in range(4):
            part = packed[16 * g:16 * g + 16]
            part = pltpu.roll(part, 4 * g, 1) if g else part
            pos = lax.rem(lane[0:16] + (128 - 4 * g), 128)
            corner = (pos < 2) | ((pos >= 62) & (pos < 66)) | (pos >= 126)
            fold = jnp.where(corner, part, fold)
        cpack[...] = fold

    def unfold(folded):
        return jnp.concatenate([folded] + [pltpu.roll(folded, 128 - 4 * g, 1) for g in range(1, 4)], axis=0)

    def halo_copies(buf, epack, cpack, erecv, crecv, ss, rs):
        row = lambda p: buf.at[pl.ds((p * 3 + 1) * 64, 64)]
        plan = [
            (cpack, crecv.at[0], (south, east)),
            (cpack, crecv.at[1], (south, west)),
            (cpack, crecv.at[2], (north, east)),
            (cpack, crecv.at[3], (north, west)),
            (row(1), row(33), (north, lon)),
            (row(32), row(0), (south, lon)),
            (epack, erecv.at[0], (lat, east)),
            (epack, erecv.at[1], (lat, west)),
        ]
        return [
            pltpu.make_async_remote_copy(
                src_ref=s, dst_ref=d, send_sem=ss.at[k], recv_sem=rs.at[k], device_id=t, device_id_type=MESH
            )
            for k, (s, d, t) in enumerate(plan)
        ]

    def insert(buf, p, b, joined, q):
        half = pl.ds(b * 128, 128)
        base = p * 192
        r = pltpu.roll(joined, (127 - 2 * q) % 128, 1)
        buf[base:base + 64, half] = jnp.where(lane == 0, r, buf[base:base + 64, half])
        buf[base + 128:base + 192, half] = jnp.where(lane == 127, r, buf[base + 128:base + 192, half])

    def join(left, right):
        return jnp.where(lax.rem(lane, 2) == 0, pltpu.roll(right, 127, 1), pltpu.roll(left, 1, 1))

    def finish_rows(buf, crecv):
        for p, keep in ((0, lat > 0), (33, lat < 15)):
            base = p * 192
            scale = jnp.where(keep, 1.0, 0.0).astype(F32)
            v = (buf[base + 64:base + 128, :].astype(F32) * scale).astype(BF)
            buf[base + 64:base + 128, :] = v
            for b in range(2):
                half = pl.ds(b * 128, 128)
                vb = v[:, b * 128:(b + 1) * 128]
                buf[base:base + 64, half] = pltpu.roll(vb, 1, 1)
                buf[base + 128:base + 192, half] = pltpu.roll(vb, 127, 1)
            left, right, i = (crecv[0], crecv[1], 31) if p == 0 else (crecv[2], crecv[3], 0)
            corner = (join(unfold(left), unfold(right)).astype(F32) * scale).astype(BF)
            for b in range(2):
                insert(buf, p, b, corner, b * 32 + i)

    def finish_columns(buf, erecv):
        joined = join(erecv[0], erecv[1])
        for b in range(2):
            for i in range(32):
                insert(buf, i + 1, b, joined, b * 32 + i)

    def exchange(src, buf, sem):
        for f in OFFSETS:
            pltpu.make_async_remote_copy(
                src_ref=src, dst_ref=buf.at[me], send_sem=gss.at[sem], recv_sem=grs.at[sem],
                device_id=peer(f), device_id_type=MESH,
            ).start()

    def exchange_wait(buf, sem):
        pltpu.make_async_copy(buf.at[pl.ds(0, 127)], buf.at[pl.ds(0, 127)], grs.at[sem]).wait()

    def exchange_sent(buf, sem):
        pltpu.make_async_copy(buf.at[pl.ds(0, 127)], buf.at[pl.ds(0, 127)], gss.at[sem]).wait()

    loads[0].wait()
    for b in range(2):
        t = jnp.transpose(xin[b] * mask_bf[None], (1, 0, 2))
        for i in range(32):
            xs[(i + 1) * 192 + 64:(i + 1) * 192 + 128, b * 128:(b + 1) * 128] = t[i]
    shifts_and_pack(xs, epx, cpx)

    pl.semaphore_wait(barrier, len(GREETED))
    halo_x = halo_copies(xs, epx, cpx, erx, crx, hsx, hrx)
    for c in halo_x:
        c.start()
    count_src[...] = jnp.broadcast_to(n_local, (1, 128))

    def count_line(src, buf, at, line, sem):
        for there in line:
            pltpu.make_async_remote_copy(
                src_ref=src, dst_ref=buf.at[at], send_sem=cns.at[sem], recv_sem=cnr.at[sem],
                device_id=there, device_id_type=MESH,
            ).start()
        buf[at] = src[...]

    count_line(count_src, count_lon, lon, [(lat, lax.rem(lon + b, 8)) for a, b in GREETED if b and not a], 0)
    for a, b in GREETED:
        if a and not b:
            pl.semaphore_signal(all_here, 1, device_id=(lax.rem(lat + a, 16), lon), device_id_type=MESH)
    loads[5].wait()
    for b in range(2):
        t = jnp.transpose(cin[b] * mask_bf[None], (1, 0, 2))
        for i in range(32):
            ctm[i * 64:(i + 1) * 64, b * 128:(b + 1) * 128] = t[i]
    near = jnp.zeros((64, 128), F32)
    for p in range(16):
        if p == 0:
            r = jnp.dot(wf[:, 192:768], xs[192:768, :], preferred_element_type=F32)
        elif p == 15:
            r = jnp.dot(wf[:, 0:576], xs[30 * 192:33 * 192, :], preferred_element_type=F32)
        else:
            r = jnp.dot(wf[...], xs[p * 384:p * 384 + 768, :], preferred_element_type=F32)
        cv[p * 128:(p + 1) * 128, :] = r
        for h in range(2):
            m = mrow[2 * p + h:2 * p + h + 1, :]
            near = near + (r[h * 64:(h + 1) * 64, :128] + r[h * 64:(h + 1) * 64, 128:]) * m
    n_safe = jnp.maximum(n_local, 1.0)
    pivot = jnp.broadcast_to(jnp.sum(near, axis=1, keepdims=True) / n_safe, (64, 128))
    pivot_row = jnp.transpose(jnp.concatenate([pivot, jnp.zeros((64, 128), F32)], axis=0), (1, 0))[0:1]

    pltpu.make_async_copy(count_lon.at[pl.ds(0, 7)], count_lon.at[pl.ds(0, 7)], cnr.at[0]).wait()
    sixteenth = lax.div(lax.broadcasted_iota(jnp.int32, (1, 128), 1), 16)
    line = count_lon[0]
    for k in range(1, 8):
        line = jnp.where(sixteenth == k, count_lon[k], line)
    count_row[...] = line
    count_line(count_row, count_lat, lat, [(lax.rem(lat + a, 16), lon) for a, b in GREETED if a and not b], 1)

    for c in halo_x:
        c.wait()
    finish_rows(xs, crx)
    top = jnp.dot(wrow[0:64, :], xs[0:192, :], preferred_element_type=F32)
    bottom = jnp.dot(wrow[64:128, :], xs[33 * 192:34 * 192, :], preferred_element_type=F32)
    joined = join(erx[0], erx[1])
    place = lax.rem(lax.div(lane, 2), 32)
    nothing = jnp.zeros((64, 128), BF)
    above = jnp.where(place == 0, nothing, pltpu.roll(joined, 2, 1))
    below = jnp.where(place == 31, nothing, pltpu.roll(joined, 126, 1))
    sides = jnp.dot(wcol[...], jnp.concatenate([above, joined, below], axis=0), preferred_element_type=F32)
    sides = jnp.where(lax.rem(lane, 2) == 0, sides[0:64], sides[64:128])
    edge = jnp.logical_or(lane == 0, lane == 127)
    first = jnp.zeros((64, 128), F32)
    second = jnp.zeros((64, 128), F32)
    for i in range(32):
        m = mrow[i:i + 1, :]
        for b in range(2):
            at = (pl.ds(i * 64, 64), pl.ds(b * 128, 128))
            side = pltpu.roll(sides, (127 - 2 * (b * 32 + i)) % 128, 1)
            v = cv[at] + jnp.where(edge, side, 0.0)
            if i == 0:
                v = v + top[:, b * 128:(b + 1) * 128]
            if i == 31:
                v = v + bottom[:, b * 128:(b + 1) * 128]
            cv[at] = v
            d = v - pivot
            md = d * m
            first = first + md
            second = second + d * md
    row = jnp.sum(jnp.transpose(jnp.concatenate([first, second], axis=0), (1, 0)), axis=0, keepdims=True)
    low = lax.broadcasted_iota(jnp.int32, (1, 128), 1) < 64
    sums_here = pltpu.roll(row, 64, 1)
    row = jnp.where(low, row + n_local * pivot_row, row - sums_here * sums_here / n_safe)
    stat_src[...] = row
    pl.semaphore_wait(all_here, 15)
    exchange(stat_src, stat_buf, 0)
    stat_buf[me] = stat_src[...]
    pltpu.make_async_copy(count_lat.at[pl.ds(0, 15)], count_lat.at[pl.ds(0, 15)], cnr.at[1]).wait()
    own_part = lax.div(lax.broadcasted_iota(jnp.int32, (8, 128), 1), 16) == lax.broadcasted_iota(jnp.int32, (8, 128), 0)
    counts = []
    for k in range(16):
        one = jnp.where(own_part, jnp.broadcast_to(count_lat[k], (8, 128)), 0.0)
        one = jnp.sum(one, axis=1, keepdims=True) * 0.0625
        counts.append(jnp.broadcast_to(one, (8, 128)))
    counts = jnp.concatenate(counts, axis=0)
    count = jnp.maximum(jnp.sum(counts, axis=0, keepdims=True), 1.0)
    weights = 1.0 / jnp.maximum(counts, 1.0)
    finish_columns(xs, erx)
    exchange_wait(stat_buf, 0)
    sums = stat_buf[:, 0, :]
    total = jnp.sum(sums, axis=0, keepdims=True)
    mean = total / count
    apart = sums * weights - mean
    between = jnp.sum(apart * apart * counts, axis=0, keepdims=True)
    var = (total + pltpu.roll(between, 64, 1)) / count
    mi = column(jnp.where(low, mean, lax.rsqrt(var + 1e-05)))
    cols[128:256, :] = mi

    mean_c, inv_c, gain_c, bias_c = cols[128:192, :], cols[192:256, :], cols[0:64, :], cols[64:128, :]
    gsum = jnp.zeros((64, 128), F32)
    bsum = jnp.zeros((64, 128), F32)
    for i in range(32):
        for b in range(2):
            at = (pl.ds(i * 64, 64), pl.ds(b * 128, 128))
            xhat = (cv[at] - mean_c) * inv_c
            pre = gain_c * xhat + bias_c
            s = 0.5 * jnp.tanh(0.5 * pre) + 0.5
            d = ctm[at].astype(F32) * (s * (1.0 + pre * (1.0 - s)))
            dp[at] = d
            bsum = bsum + d
            gsum = gsum + d * xhat
    grad_src[...] = jnp.sum(jnp.transpose(jnp.concatenate([bsum, gsum], axis=0), (1, 0)), axis=0, keepdims=True)
    exchange(grad_src, grad_buf, 1)
    grad_buf[me] = grad_src[...]

    def native(src, b):
        t = src[:, b * 128:(b + 1) * 128].reshape(32, 64, 128)
        return jnp.transpose(t, (1, 0, 2)) * mask_bf[None]

    for i in range(32):
        for b in range(2):
            at = (pl.ds(i * 64, 64), pl.ds(b * 128, 128))
            pre = gain_c * ((cv[at] - mean_c) * inv_c) + bias_c
            actt[at] = (pre * (0.5 * jnp.tanh(0.5 * pre) + 0.5)).astype(BF)
    for b in range(2):
        aout[b] = native(actt, b)

    exchange_wait(grad_buf, 1)
    gtot = jnp.sum(grad_buf[:, 0, :], axis=0, keepdims=True)
    bias_out[...] = gtot[0, :64]
    gain_out[...] = pltpu.roll(gtot, 64, 1)[0, :64]
    sc = column(gg * gtot / count)
    cols[256:384, :] = sc
    sf_c, sg_c = cols[256:320, :], cols[320:384, :]

    def left_rows(p, kx):
        return jnp.concatenate(
            [xs[(4 * p + k) * 192 + kx * 64:(4 * p + k) * 192 + kx * 64 + 64, :] for k in range(6)], axis=0
        )

    for i in range(32):
        m = mrow[i:i + 1, :]
        for b in range(2):
            at = (pl.ds(i * 64, 64), pl.ds(b * 128, 128))
            xhat = (cv[at] - mean_c) * inv_c
            d = m * inv_c * (gain_c * dp[at] - sf_c - xhat * sg_c)
            d = d.astype(BF)
            ds[(i + 1) * 192 + 64:(i + 1) * 192 + 128, b * 128:(b + 1) * 128] = d
            rows4[i * 64:(i + 1) * 64, b * 128:(b + 1) * 128] = d
        if i % 4 == 3:
            p = i // 4
            part = lax.dot_general(
                left_rows(p, 0), rows4[p * 256:(p + 1) * 256, :], NT, preferred_element_type=F32
            )
            if p == 0:
                acc[...] = part
            else:
                acc[...] += part
    part_of = lax.rem(x + y + z, 4)
    own = part_of < 3
    mine = part_of * 32 + lat * 2 + core
    for kx in range(3):
        for p in range(8 if kx else 0):
            part = lax.dot_general(
                left_rows(p, kx), rows4[p * 256:(p + 1) * 256, :], NT, preferred_element_type=F32
            )
            if p == 0:
                acc[...] = part
            else:
                acc[...] += part
        here = []
        for ky in range(3):
            v = acc[ky * 64:(ky + 1) * 64, 0:64]
            for k in range(1, 4):
                v = v + acc[(ky + k) * 64:(ky + k + 1) * 64, k * 64:(k + 1) * 64]
            here.append(v)
        here = jnp.concatenate(here, axis=0)
        here = jnp.concatenate([here[:96], here[96:]], axis=1)
        for k in range(3):
            wsrc[kx * 32:(kx + 1) * 32, k, :] = here[32 * k:32 * k + 32]
        for dx, dy in FAR_XY:
            for dc in (1, 0):
                la = lats[dx][dy]
                pc = lax.rem(core + dc, 2)
                lo = lax.rem(kx + 8 - xs_at[dx] - ys_at[dy], 4) * 2 + pc
                block = kx * 32 + la * 2 + pc
                send = pltpu.make_async_remote_copy(
                    src_ref=wsrc.at[block], dst_ref=wbuf.at[me], send_sem=gss.at[2], recv_sem=grs.at[2],
                    device_id=(la, lo), device_id_type=MESH,
                )
                if dx or dy or dc:
                    send.start()
                else:
                    pl.when(part_of != kx)(send.start)

    @pl.when(own)
    def _():
        wbuf[me] = wsrc[mine]

    shifts_and_pack(ds, epd, cpd)
    halo_d = halo_copies(ds, epd, cpd, erd, crd, hsd, hrd)
    for c in halo_d:
        c.start()
    @pl.when(own)
    def _():
        pltpu.make_async_copy(wbuf.at[pl.ds(0, 127)], wbuf.at[pl.ds(0, 127)], grs.at[2]).wait()
        quarters = [jnp.sum(wbuf[32 * k:32 * k + 32], axis=0) for k in range(4)]
        wgat[mine] = (quarters[0] + quarters[1]) + (quarters[2] + quarters[3])
        for f in OFFSETS:
            pltpu.make_async_remote_copy(
                src_ref=wgat.at[mine], dst_ref=wgat.at[mine], send_sem=gss.at[3], recv_sem=grs.at[3],
                device_id=peer(f), device_id_type=MESH,
            ).start()

    for c in halo_d:
        c.wait()
    finish_rows(ds, crd)
    finish_columns(ds, erd)
    for p in range(16):
        r = jnp.dot(wb[...], ds[p * 384:p * 384 + 768, :], preferred_element_type=F32)
        actt[p * 128:(p + 1) * 128, :] = r.astype(BF)
    for b in range(2):
        sout[b] = native(actt, b)

    @pl.when(own)
    def _():
        pltpu.make_async_copy(wsrc.at[pl.ds(0, 95)], wsrc.at[pl.ds(0, 95)], gss.at[2]).wait()
        pltpu.make_async_copy(wgat.at[pl.ds(0, 95)], wgat.at[pl.ds(0, 95)], grs.at[3]).wait()
        pltpu.make_async_copy(wbuf.at[pl.ds(0, 127)], wbuf.at[pl.ds(0, 127)], gss.at[3]).wait()

    @pl.when(jnp.logical_not(own))
    def _():
        pltpu.make_async_copy(wsrc, wsrc, gss.at[2]).wait()
        pltpu.make_async_copy(wgat, wgat, grs.at[3]).wait()

    exchange_sent(stat_buf, 0)
    exchange_sent(grad_buf, 1)
    pltpu.make_async_copy(count_lon.at[pl.ds(0, 7)], count_lon.at[pl.ds(0, 7)], cns.at[0]).wait()
    pltpu.make_async_copy(count_lat.at[pl.ds(0, 15)], count_lat.at[pl.ds(0, 15)], cns.at[1]).wait()
    for kx in range(3):
        w = jnp.concatenate([wgat[kx * 32:(kx + 1) * 32, k, :] for k in range(3)], axis=0)
        w = jnp.concatenate([w[:, :64], w[:, 64:]], axis=0)
        for ky in range(3):
            wgrad_out[ky, kx] = w[ky * 64:(ky + 1) * 64]


def store(*refs):
    copies = [pltpu.make_async_copy(refs[k], refs[k + 5], refs[10].at[k]) for k in range(5)]
    for c in copies:
        c.start()
    for c in copies:
        c.wait()


def on_device(state, land_mask, conv_weight, norm_gain, batchnorm_bias, cotangent):
    vm = pl.BlockSpec(memory_space=pltpu.VMEM)
    hbm = pl.BlockSpec(memory_space=pltpu.HBM)
    anywhere = pl.BlockSpec(memory_space=pl.ANY)
    S = jax.ShapeDtypeStruct
    big = (2, 64, 32, 128)
    outs = [S(big, BF), S(big, BF), S((3, 3, 64, 64), F32), S((64,), F32), S((64,), F32)]
    V = pltpu.VMEM
    made = pl.pallas_call(
        kernel,
        out_shape=outs,
        in_specs=[hbm] * 6,
        out_specs=[vm] * 5,
        scratch_shapes=[
            V(big, BF), V(big, BF), V((32, 128), jnp.int32), V((3, 3, 64, 64), BF), V((64,), F32), V((64,), F32),
            V((34 * 192, 256), BF), V((34 * 192, 256), BF),
            V((2048, 256), F32), V((2048, 256), F32), V((2048, 256), BF), V((2048, 256), BF),
            V((128, 768), BF), V((128, 768), BF), V((128, 192), BF), V((128, 192), BF), V((2048, 256), BF),
            V((64, 128), BF), V((64, 128), BF), V((2, 64, 128), BF), V((2, 64, 128), BF),
            V((16, 128), BF), V((16, 128), BF), V((4, 16, 128), BF), V((4, 16, 128), BF),
            V((1, 128), F32), V((128, 1, 128), F32), V((1, 128), F32), V((128, 1, 128), F32),
            V((96, 3, 128), F32), V((128, 3, 128), F32), V((384, 256), F32), V((96, 3, 128), F32),
            V((384, 128), F32), V((32, 128), F32),
            V((1, 128), F32), V((1, 128), F32), V((8, 1, 128), F32), V((16, 1, 128), F32),
            pltpu.SemaphoreType.DMA((6,)),
            pltpu.SemaphoreType.DMA((8,)), pltpu.SemaphoreType.DMA((8,)),
            pltpu.SemaphoreType.DMA((8,)), pltpu.SemaphoreType.DMA((8,)),
            pltpu.SemaphoreType.DMA((4,)), pltpu.SemaphoreType.DMA((4,)),
            pltpu.SemaphoreType.DMA((2,)), pltpu.SemaphoreType.DMA((2,)),
            pltpu.SemaphoreType.REGULAR,
        ],
        compiler_params=pltpu.CompilerParams(
            collective_id=0, has_side_effects=True, vmem_limit_bytes=40 * 2**20
        ),
    )(*[pltpu.with_memory_space_constraint(a, pltpu.HBM) for a in (state, land_mask, conv_weight, norm_gain, batchnorm_bias, cotangent)])
    return pl.pallas_call(
        store,
        out_shape=outs,
        in_specs=[vm] * 5,
        out_specs=[anywhere] * 5,
        scratch_shapes=[pltpu.SemaphoreType.DMA((5,))],
    )(*[pltpu.with_memory_space_constraint(a, pltpu.VMEM) for a in made])


def solution(mesh):
    return jax.shard_map(
        on_device,
        mesh=mesh,
        in_specs=(
            P(None, None, "lat", "lon"),
            P("lat", "lon"),
            P(),
            P(),
            P(),
            P(None, None, "lat", "lon"),
        ),
        out_specs=(P(None, None, "lat", "lon"), P(None, None, "lat", "lon"), P(), P(), P()),
        check_vma=False,
    )
```

```python
import jax
import jax.numpy as jnp
from jax import lax
from jax.experimental import pallas as pl
from jax.experimental.pallas import tpu as pltpu
from jax.sharding import PartitionSpec as P

BF = jnp.bfloat16
F32 = jnp.float32
MESH = pl.DeviceIdType.MESH
NT = (((1,), (1,)), ((), ()))


def peer_offsets():
    found = []
    for dx in range(4):
        for dy in range(4):
            for dz in range(4):
                for dc in range(2):
                    if dx or dy or dz or dc:
                        hops = sum(min(a, 4 - a) for a in (dx, dy, dz))
                        found.append((-hops, dx, dy, dz, dc))
    found.sort()
    return [t[1:] for t in found]


OFFSETS = peer_offsets()
FAR_XY = [(2, 2), (2, 1), (2, 3), (1, 2), (3, 2), (2, 0), (0, 2), (1, 1), (1, 3), (3, 1), (3, 3), (1, 0), (3, 0), (0, 1), (0, 3), (0, 0)]
GREETED = [(a, 0) for a in (10, 6, 2, 14, 9, 11, 5, 7, 8, 1, 3, 13, 15, 4, 12)]
GREETED = [(1, 1), (1, 7), (15, 1), (15, 7)] + GREETED + [(0, b) for b in (4, 5, 3, 2, 6, 1, 7)]


def kernel(
    state, mask_hbm, weight_hbm, gain_hbm, bias_hbm, cot,
    aout, sout, wgrad_out, gain_out, bias_out,
    xin, cin, mask, weight, gain, bias, xs, ds, cv, dp, ctm, actt, wf, wb, wrow, wcol, rows4, epx, epd, erx, erd, cpx, cpd, crx, crd,
    stat_src, stat_buf, grad_src, grad_buf, wsrc, wbuf, accs, wgat, cols, mrow,
    count_src, count_row, count_lon, count_lat,
    dma, hsx, hrx, hsd, hrd, gss, grs, cns, cnr, all_here,
):
    lat = lax.axis_index("lat")
    lon = lax.axis_index("lon")
    me = lat * 8 + lon
    x, y, z, core = lax.div(lat, 4), lax.rem(lat, 4), lax.div(lon, 2), lax.rem(lon, 2)
    xs_at = [lax.rem(x + d, 4) for d in range(4)]
    ys_at = [lax.rem(y + d, 4) for d in range(4)]
    lats = [[xs_at[dx] * 4 + ys_at[dy] for dy in range(4)] for dx in range(4)]
    lons = [[lax.rem(z + d, 4) * 2 + lax.rem(core + c, 2) for c in range(2)] for d in range(4)]

    def peer(offset):
        dx, dy, dz, dc = offset
        return lats[dx][dy], lons[dz][dc]

    north, south = lax.rem(lat + 15, 16), lax.rem(lat + 1, 16)
    west, east = lax.rem(lon + 7, 8), lax.rem(lon + 1, 8)

    loads = [
        pltpu.make_async_copy(s, d, dma.at[k])
        for k, (s, d) in enumerate(
            [(state, xin), (mask_hbm, mask), (weight_hbm, weight), (gain_hbm, gain), (bias_hbm, bias), (cot, cin)]
        )
    ]
    for c in loads:
        c.start()
    barrier = pltpu.get_barrier_semaphore()
    for a, b in GREETED:
        there = (lax.rem(lat + a, 16), lax.rem(lon + b, 8))
        pl.semaphore_signal(barrier, 1, device_id=there, device_id_type=MESH)

    for c in loads[1:5]:
        c.wait()
    maskf = mask[...].astype(F32)
    mrow[...] = maskf
    mask_bf = maskf.astype(BF)
    n_local = 2.0 * jnp.sum(jnp.sum(maskf, axis=0, keepdims=True), axis=1, keepdims=True)

    taps = weight[...].reshape(576, 64)
    wt = jnp.transpose(taps.astype(F32), (1, 0)).astype(BF)
    zero = jnp.zeros((64, 192), BF)
    wrow[0:64, :] = wt[:, 0:192]
    wrow[64:128, :] = wt[:, 384:576]
    wcol[0:64, :] = jnp.concatenate([wt[:, 192 * k + 128:192 * k + 192] for k in range(3)], axis=1)
    wcol[64:128, :] = jnp.concatenate([wt[:, 192 * k:192 * k + 64] for k in range(3)], axis=1)
    wf[0:64, :] = jnp.concatenate([wt, zero], axis=1)
    wf[64:128, :] = jnp.concatenate([zero, wt], axis=1)
    back = jnp.concatenate([weight[2 - t // 3, 2 - t % 3] for t in range(9)], axis=1)
    wb[0:64, :] = jnp.concatenate([back, zero], axis=1)
    wb[64:128, :] = jnp.concatenate([zero, back], axis=1)
    gb = jnp.concatenate([gain[...].reshape(1, 64), bias[...].reshape(1, 64)], axis=1)
    gg = jnp.concatenate([gain[...].reshape(1, 64), gain[...].reshape(1, 64)], axis=1)

    def column(row):
        return jnp.transpose(jnp.broadcast_to(row, (128, 128)), (1, 0))

    gbc = column(gb)
    cols[0:128, :] = gbc

    lane = lax.broadcasted_iota(jnp.int32, (64, 128), 1)

    def shifts_and_pack(buf, epack, cpack):
        packed = jnp.zeros((64, 128), BF)
        none = jnp.zeros((64, 128), BF)
        for b in range(2):
            half = pl.ds(b * 128, 128)
            for i in range(32):
                q = b * 32 + i
                base = (i + 1) * 192
                v = buf[base + 64:base + 128, half]
                buf[base:base + 64, half] = jnp.where(lane == 0, none, pltpu.roll(v, 1, 1))
                buf[base + 128:base + 192, half] = jnp.where(lane == 127, none, pltpu.roll(v, 127, 1))
                turned = pltpu.roll(v, (2 * q + 1) % 128, 1)
                packed = jnp.where(lax.div(lane, 2) == q, turned, packed)
        epack[...] = packed
        fold = jnp.zeros((16, 128), BF)
        for g in range(4):
            part = packed[16 * g:16 * g + 16]
            part = pltpu.roll(part, 4 * g, 1) if g else part
            pos = lax.rem(lane[0:16] + (128 - 4 * g), 128)
            corner = (pos < 2) | ((pos >= 62) & (pos < 66)) | (pos >= 126)
            fold = jnp.where(corner, part, fold)
        cpack[...] = fold

    def unfold(folded):
        return jnp.concatenate([folded] + [pltpu.roll(folded, 128 - 4 * g, 1) for g in range(1, 4)], axis=0)

    def halo_copies(buf, epack, cpack, erecv, crecv, ss, rs):
        row = lambda p: buf.at[pl.ds((p * 3 + 1) * 64, 64)]
        plan = [
            (cpack, crecv.at[0], (south, east)),
            (cpack, crecv.at[1], (south, west)),
            (cpack, crecv.at[2], (north, east)),
            (cpack, crecv.at[3], (north, west)),
            (row(1), row(33), (north, lon)),
            (row(32), row(0), (south, lon)),
            (epack, erecv.at[0], (lat, east)),
            (epack, erecv.at[1], (lat, west)),
        ]
        return [
            pltpu.make_async_remote_copy(
                src_ref=s, dst_ref=d, send_sem=ss.at[k], recv_sem=rs.at[k], device_id=t, device_id_type=MESH
            )
            for k, (s, d, t) in enumerate(plan)
        ]

    def insert(buf, p, b, joined, q):
        half = pl.ds(b * 128, 128)
        base = p * 192
        r = pltpu.roll(joined, (127 - 2 * q) % 128, 1)
        buf[base:base + 64, half] = jnp.where(lane == 0, r, buf[base:base + 64, half])
        buf[base + 128:base + 192, half] = jnp.where(lane == 127, r, buf[base + 128:base + 192, half])

    def join(left, right):
        return jnp.where(lax.rem(lane, 2) == 0, pltpu.roll(right, 127, 1), pltpu.roll(left, 1, 1))

    def finish_rows(buf, crecv):
        for p, keep in ((0, lat > 0), (33, lat < 15)):
            base = p * 192
            scale = jnp.where(keep, 1.0, 0.0).astype(F32)
            v = (buf[base + 64:base + 128, :].astype(F32) * scale).astype(BF)
            buf[base + 64:base + 128, :] = v
            for b in range(2):
                half = pl.ds(b * 128, 128)
                vb = v[:, b * 128:(b + 1) * 128]
                buf[base:base + 64, half] = pltpu.roll(vb, 1, 1)
                buf[base + 128:base + 192, half] = pltpu.roll(vb, 127, 1)
            left, right, i = (crecv[0], crecv[1], 31) if p == 0 else (crecv[2], crecv[3], 0)
            corner = (join(unfold(left), unfold(right)).astype(F32) * scale).astype(BF)
            for b in range(2):
                insert(buf, p, b, corner, b * 32 + i)

    def finish_columns(buf, erecv):
        joined = join(erecv[0], erecv[1])
        for b in range(2):
            for i in range(32):
                insert(buf, i + 1, b, joined, b * 32 + i)

    def exchange(src, buf, sem):
        for f in OFFSETS:
            pltpu.make_async_remote_copy(
                src_ref=src, dst_ref=buf.at[me], send_sem=gss.at[sem], recv_sem=grs.at[sem],
                device_id=peer(f), device_id_type=MESH,
            ).start()

    def exchange_wait(buf, sem):
        pltpu.make_async_copy(buf.at[pl.ds(0, 127)], buf.at[pl.ds(0, 127)], grs.at[sem]).wait()

    def exchange_sent(buf, sem):
        pltpu.make_async_copy(buf.at[pl.ds(0, 127)], buf.at[pl.ds(0, 127)], gss.at[sem]).wait()

    loads[0].wait()
    for b in range(2):
        t = jnp.transpose(xin[b] * mask_bf[None], (1, 0, 2))
        for i in range(32):
            xs[(i + 1) * 192 + 64:(i + 1) * 192 + 128, b * 128:(b + 1) * 128] = t[i]
    shifts_and_pack(xs, epx, cpx)

    pl.semaphore_wait(barrier, len(GREETED))
    halo_x = halo_copies(xs, epx, cpx, erx, crx, hsx, hrx)
    for c in halo_x:
        c.start()
    count_src[...] = jnp.broadcast_to(n_local, (1, 128))

    def count_line(src, buf, at, line, sem):
        for there in line:
            pltpu.make_async_remote_copy(
                src_ref=src, dst_ref=buf.at[at], send_sem=cns.at[sem], recv_sem=cnr.at[sem],
                device_id=there, device_id_type=MESH,
            ).start()
        buf[at] = src[...]

    count_line(count_src, count_lon, lon, [(lat, lax.rem(lon + b, 8)) for a, b in GREETED if b and not a], 0)
    for a, b in GREETED:
        if a and not b:
            pl.semaphore_signal(all_here, 1, device_id=(lax.rem(lat + a, 16), lon), device_id_type=MESH)
    loads[5].wait()
    for b in range(2):
        t = jnp.transpose(cin[b] * mask_bf[None], (1, 0, 2))
        for i in range(32):
            ctm[i * 64:(i + 1) * 64, b * 128:(b + 1) * 128] = t[i]
    near = jnp.zeros((64, 128), F32)
    for p in range(16):
        if p == 0:
            r = jnp.dot(wf[:, 192:768], xs[192:768, :], preferred_element_type=F32)
        elif p == 15:
            r = jnp.dot(wf[:, 0:576], xs[30 * 192:33 * 192, :], preferred_element_type=F32)
        else:
            r = jnp.dot(wf[...], xs[p * 384:p * 384 + 768, :], preferred_element_type=F32)
        cv[p * 128:(p + 1) * 128, :] = r
        for h in range(2):
            m = mrow[2 * p + h:2 * p + h + 1, :]
            near = near + (r[h * 64:(h + 1) * 64, :128] + r[h * 64:(h + 1) * 64, 128:]) * m
    n_safe = jnp.maximum(n_local, 1.0)
    pivot = jnp.broadcast_to(jnp.sum(near, axis=1, keepdims=True) / n_safe, (64, 128))
    pivot_row = jnp.transpose(jnp.concatenate([pivot, jnp.zeros((64, 128), F32)], axis=0), (1, 0))[0:1]

    pltpu.make_async_copy(count_lon.at[pl.ds(0, 7)], count_lon.at[pl.ds(0, 7)], cnr.at[0]).wait()
    sixteenth = lax.div(lax.broadcasted_iota(jnp.int32, (1, 128), 1), 16)
    line = count_lon[0]
    for k in range(1, 8):
        line = jnp.where(sixteenth == k, count_lon[k], line)
    count_row[...] = line
    count_line(count_row, count_lat, lat, [(lax.rem(lat + a, 16), lon) for a, b in GREETED if a and not b], 1)

    for c in halo_x:
        c.wait()
    finish_rows(xs, crx)
    top = jnp.dot(wrow[0:64, :], xs[0:192, :], preferred_element_type=F32)
    bottom = jnp.dot(wrow[64:128, :], xs[33 * 192:34 * 192, :], preferred_element_type=F32)
    joined = join(erx[0], erx[1])
    place = lax.rem(lax.div(lane, 2), 32)
    nothing = jnp.zeros((64, 128), BF)
    above = jnp.where(place == 0, nothing, pltpu.roll(joined, 2, 1))
    below = jnp.where(place == 31, nothing, pltpu.roll(joined, 126, 1))
    sides = jnp.dot(wcol[...], jnp.concatenate([above, joined, below], axis=0), preferred_element_type=F32)
    sides = jnp.where(lax.rem(lane, 2) == 0, sides[0:64], sides[64:128])
    edge = jnp.logical_or(lane == 0, lane == 127)
    first = jnp.zeros((64, 128), F32)
    second = jnp.zeros((64, 128), F32)
    for i in range(32):
        m = mrow[i:i + 1, :]
        for b in range(2):
            at = (pl.ds(i * 64, 64), pl.ds(b * 128, 128))
            side = pltpu.roll(sides, (127 - 2 * (b * 32 + i)) % 128, 1)
            v = cv[at] + jnp.where(edge, side, 0.0)
            if i == 0:
                v = v + top[:, b * 128:(b + 1) * 128]
            if i == 31:
                v = v + bottom[:, b * 128:(b + 1) * 128]
            cv[at] = v
            d = v - pivot
            md = d * m
            first = first + md
            second = second + d * md
    row = jnp.sum(jnp.transpose(jnp.concatenate([first, second], axis=0), (1, 0)), axis=0, keepdims=True)
    low = lax.broadcasted_iota(jnp.int32, (1, 128), 1) < 64
    sums_here = pltpu.roll(row, 64, 1)
    row = jnp.where(low, row + n_local * pivot_row, row - sums_here * sums_here / n_safe)
    stat_src[...] = row
    pl.semaphore_wait(all_here, 15)
    exchange(stat_src, stat_buf, 0)
    stat_buf[me] = stat_src[...]
    pltpu.make_async_copy(count_lat.at[pl.ds(0, 15)], count_lat.at[pl.ds(0, 15)], cnr.at[1]).wait()
    own_part = lax.div(lax.broadcasted_iota(jnp.int32, (8, 128), 1), 16) == lax.broadcasted_iota(jnp.int32, (8, 128), 0)
    counts = []
    for k in range(16):
        one = jnp.where(own_part, jnp.broadcast_to(count_lat[k], (8, 128)), 0.0)
        one = jnp.sum(one, axis=1, keepdims=True) * 0.0625
        counts.append(jnp.broadcast_to(one, (8, 128)))
    counts = jnp.concatenate(counts, axis=0)
    count = jnp.maximum(jnp.sum(counts, axis=0, keepdims=True), 1.0)
    weights = 1.0 / jnp.maximum(counts, 1.0)
    finish_columns(xs, erx)
    exchange_wait(stat_buf, 0)
    sums = stat_buf[:, 0, :]
    total = jnp.sum(sums, axis=0, keepdims=True)
    mean = total / count
    apart = sums * weights - mean
    between = jnp.sum(apart * apart * counts, axis=0, keepdims=True)
    var = (total + pltpu.roll(between, 64, 1)) / count
    mi = column(jnp.where(low, mean, lax.rsqrt(var + 1e-05)))
    cols[128:256, :] = mi

    mean_c, inv_c, gain_c, bias_c = cols[128:192, :], cols[192:256, :], cols[0:64, :], cols[64:128, :]
    gsum = jnp.zeros((64, 128), F32)
    bsum = jnp.zeros((64, 128), F32)
    for i in range(32):
        for b in range(2):
            at = (pl.ds(i * 64, 64), pl.ds(b * 128, 128))
            xhat = (cv[at] - mean_c) * inv_c
            pre = gain_c * xhat + bias_c
            s = 0.5 * jnp.tanh(0.5 * pre) + 0.5
            d = ctm[at].astype(F32) * (s * (1.0 + pre * (1.0 - s)))
            dp[at] = d
            bsum = bsum + d
            gsum = gsum + d * xhat
    grad_src[...] = jnp.sum(jnp.transpose(jnp.concatenate([bsum, gsum], axis=0), (1, 0)), axis=0, keepdims=True)
    exchange(grad_src, grad_buf, 1)
    grad_buf[me] = grad_src[...]

    def native(src, b):
        t = src[:, b * 128:(b + 1) * 128].reshape(32, 64, 128)
        return jnp.transpose(t, (1, 0, 2)) * mask_bf[None]

    for i in range(32):
        for b in range(2):
            at = (pl.ds(i * 64, 64), pl.ds(b * 128, 128))
            pre = gain_c * ((cv[at] - mean_c) * inv_c) + bias_c
            actt[at] = (pre * (0.5 * jnp.tanh(0.5 * pre) + 0.5)).astype(BF)
    for b in range(2):
        aout[b] = native(actt, b)

    exchange_wait(grad_buf, 1)
    gtot = jnp.sum(grad_buf[:, 0, :], axis=0, keepdims=True)
    bias_out[...] = gtot[0, :64]
    gain_out[...] = pltpu.roll(gtot, 64, 1)[0, :64]
    sc = column(gg * gtot / count)
    cols[256:384, :] = sc
    sf_c, sg_c = cols[256:320, :], cols[320:384, :]

    def left_rows(p, kx):
        return jnp.concatenate(
            [xs[(4 * p + k) * 192 + kx * 64:(4 * p + k) * 192 + kx * 64 + 64, :] for k in range(6)], axis=0
        )

    for i in range(32):
        m = mrow[i:i + 1, :]
        for b in range(2):
            at = (pl.ds(i * 64, 64), pl.ds(b * 128, 128))
            xhat = (cv[at] - mean_c) * inv_c
            d = m * inv_c * (gain_c * dp[at] - sf_c - xhat * sg_c)
            d = d.astype(BF)
            ds[(i + 1) * 192 + 64:(i + 1) * 192 + 128, b * 128:(b + 1) * 128] = d
            rows4[i * 64:(i + 1) * 64, b * 128:(b + 1) * 128] = d
        if i % 4 == 3:
            p = i // 4
            for kx in range(2):
                part = lax.dot_general(
                    left_rows(p, kx), rows4[p * 256:(p + 1) * 256, :], NT, preferred_element_type=F32
                )
                if p == 0:
                    accs[kx] = part
                else:
                    accs[kx] += part
    part_of = lax.rem(x + y + z, 4)
    own = part_of < 3
    mine = part_of * 32 + lat * 2 + core
    for kx in range(3):
        acc = accs.at[kx]
        for p in range(8 if kx == 2 else 0):
            part = lax.dot_general(
                left_rows(p, kx), rows4[p * 256:(p + 1) * 256, :], NT, preferred_element_type=F32
            )
            if p == 0:
                acc[...] = part
            else:
                acc[...] += part
        here = []
        for ky in range(3):
            v = acc[ky * 64:(ky + 1) * 64, 0:64]
            for k in range(1, 4):
                v = v + acc[(ky + k) * 64:(ky + k + 1) * 64, k * 64:(k + 1) * 64]
            here.append(v)
        here = jnp.concatenate(here, axis=0)
        here = jnp.concatenate([here[:96], here[96:]], axis=1)
        for k in range(3):
            wsrc[kx * 32:(kx + 1) * 32, k, :] = here[32 * k:32 * k + 32]
        for dx, dy in FAR_XY:
            for dc in (1, 0):
                la = lats[dx][dy]
                pc = lax.rem(core + dc, 2)
                lo = lax.rem(kx + 8 - xs_at[dx] - ys_at[dy], 4) * 2 + pc
                block = kx * 32 + la * 2 + pc
                send = pltpu.make_async_remote_copy(
                    src_ref=wsrc.at[block], dst_ref=wbuf.at[me], send_sem=gss.at[2], recv_sem=grs.at[2],
                    device_id=(la, lo), device_id_type=MESH,
                )
                if dx or dy or dc:
                    send.start()
                else:
                    pl.when(part_of != kx)(send.start)

    @pl.when(own)
    def _():
        wbuf[me] = wsrc[mine]

    shifts_and_pack(ds, epd, cpd)
    halo_d = halo_copies(ds, epd, cpd, erd, crd, hsd, hrd)
    for c in halo_d:
        c.start()
    @pl.when(own)
    def _():
        pltpu.make_async_copy(wbuf.at[pl.ds(0, 127)], wbuf.at[pl.ds(0, 127)], grs.at[2]).wait()
        quarters = [jnp.sum(wbuf[32 * k:32 * k + 32], axis=0) for k in range(4)]
        wgat[mine] = (quarters[0] + quarters[1]) + (quarters[2] + quarters[3])
        for f in OFFSETS:
            pltpu.make_async_remote_copy(
                src_ref=wgat.at[mine], dst_ref=wgat.at[mine], send_sem=gss.at[3], recv_sem=grs.at[3],
                device_id=peer(f), device_id_type=MESH,
            ).start()

    for c in halo_d:
        c.wait()
    finish_rows(ds, crd)
    finish_columns(ds, erd)
    for p in range(16):
        r = jnp.dot(wb[...], ds[p * 384:p * 384 + 768, :], preferred_element_type=F32)
        actt[p * 128:(p + 1) * 128, :] = r.astype(BF)
    for b in range(2):
        sout[b] = native(actt, b)

    @pl.when(own)
    def _():
        pltpu.make_async_copy(wsrc.at[pl.ds(0, 95)], wsrc.at[pl.ds(0, 95)], gss.at[2]).wait()
        pltpu.make_async_copy(wgat.at[pl.ds(0, 95)], wgat.at[pl.ds(0, 95)], grs.at[3]).wait()
        pltpu.make_async_copy(wbuf.at[pl.ds(0, 127)], wbuf.at[pl.ds(0, 127)], gss.at[3]).wait()

    @pl.when(jnp.logical_not(own))
    def _():
        pltpu.make_async_copy(wsrc, wsrc, gss.at[2]).wait()
        pltpu.make_async_copy(wgat, wgat, grs.at[3]).wait()

    exchange_sent(stat_buf, 0)
    exchange_sent(grad_buf, 1)
    pltpu.make_async_copy(count_lon.at[pl.ds(0, 7)], count_lon.at[pl.ds(0, 7)], cns.at[0]).wait()
    pltpu.make_async_copy(count_lat.at[pl.ds(0, 15)], count_lat.at[pl.ds(0, 15)], cns.at[1]).wait()
    for kx in range(3):
        w = jnp.concatenate([wgat[kx * 32:(kx + 1) * 32, k, :] for k in range(3)], axis=0)
        w = jnp.concatenate([w[:, :64], w[:, 64:]], axis=0)
        for ky in range(3):
            wgrad_out[ky, kx] = w[ky * 64:(ky + 1) * 64]


def store(*refs):
    copies = [pltpu.make_async_copy(refs[k], refs[k + 5], refs[10].at[k]) for k in range(5)]
    for c in copies:
        c.start()
    for c in copies:
        c.wait()


def on_device(state, land_mask, conv_weight, norm_gain, batchnorm_bias, cotangent):
    vm = pl.BlockSpec(memory_space=pltpu.VMEM)
    hbm = pl.BlockSpec(memory_space=pltpu.HBM)
    anywhere = pl.BlockSpec(memory_space=pl.ANY)
    S = jax.ShapeDtypeStruct
    big = (2, 64, 32, 128)
    outs = [S(big, BF), S(big, BF), S((3, 3, 64, 64), F32), S((64,), F32), S((64,), F32)]
    V = pltpu.VMEM
    made = pl.pallas_call(
        kernel,
        out_shape=outs,
        in_specs=[hbm] * 6,
        out_specs=[vm] * 5,
        scratch_shapes=[
            V(big, BF), V(big, BF), V((32, 128), jnp.int32), V((3, 3, 64, 64), BF), V((64,), F32), V((64,), F32),
            V((34 * 192, 256), BF), V((34 * 192, 256), BF),
            V((2048, 256), F32), V((2048, 256), F32), V((2048, 256), BF), V((2048, 256), BF),
            V((128, 768), BF), V((128, 768), BF), V((128, 192), BF), V((128, 192), BF), V((2048, 256), BF),
            V((64, 128), BF), V((64, 128), BF), V((2, 64, 128), BF), V((2, 64, 128), BF),
            V((16, 128), BF), V((16, 128), BF), V((4, 16, 128), BF), V((4, 16, 128), BF),
            V((1, 128), F32), V((128, 1, 128), F32), V((1, 128), F32), V((128, 1, 128), F32),
            V((96, 3, 128), F32), V((128, 3, 128), F32), V((3, 384, 256), F32), V((96, 3, 128), F32),
            V((384, 128), F32), V((32, 128), F32),
            V((1, 128), F32), V((1, 128), F32), V((8, 1, 128), F32), V((16, 1, 128), F32),
            pltpu.SemaphoreType.DMA((6,)),
            pltpu.SemaphoreType.DMA((8,)), pltpu.SemaphoreType.DMA((8,)),
            pltpu.SemaphoreType.DMA((8,)), pltpu.SemaphoreType.DMA((8,)),
            pltpu.SemaphoreType.DMA((4,)), pltpu.SemaphoreType.DMA((4,)),
            pltpu.SemaphoreType.DMA((2,)), pltpu.SemaphoreType.DMA((2,)),
            pltpu.SemaphoreType.REGULAR,
        ],
        compiler_params=pltpu.CompilerParams(
            collective_id=0, has_side_effects=True, vmem_limit_bytes=40 * 2**20
        ),
    )(*[pltpu.with_memory_space_constraint(a, pltpu.HBM) for a in (state, land_mask, conv_weight, norm_gain, batchnorm_bias, cotangent)])
    return pl.pallas_call(
        store,
        out_shape=outs,
        in_specs=[vm] * 5,
        out_specs=[anywhere] * 5,
        scratch_shapes=[pltpu.SemaphoreType.DMA((5,))],
    )(*[pltpu.with_memory_space_constraint(a, pltpu.VMEM) for a in made])


def solution(mesh):
    return jax.shard_map(
        on_device,
        mesh=mesh,
        in_specs=(
            P(None, None, "lat", "lon"),
            P("lat", "lon"),
            P(),
            P(),
            P(),
            P(None, None, "lat", "lon"),
        ),
        out_specs=(P(None, None, "lat", "lon"), P(None, None, "lat", "lon"), P(), P(), P()),
        check_vma=False,
    )
```
